32 devices in a mesh: group: 4 (over y, x), shard: 8 (over z, core).
Axes of the slice: x: 2, y: 2, z: 4, core: 2. Of those that a mesh axis runs over, the one named last changes fastest.
Arguments:
- image_states: bfloat16 [80000, 768], P(('group', 'shard')), may hold values from -6 to 6
- text_states: bfloat16 [25600, 768], P(('group', 'shard')), may hold values from -6 to 6
- image_weights: bfloat16 [768, 9216], replicated
- image_gains: float32 [2, 768], replicated, may hold values from 0.5 to 1.5
- text_weights: float32 [768, 9216], P('shard')
- text_gains: float32 [2, 768], P(None, 'shard')
- logit_scale: float32 [], replicated, may hold values from 30 to 70
- pair_ids: int32 [1600], P(('group', 'shard')), may hold values from 0 to 49, as said below
- row_stats: float32 [4, 768], P(None, 'shard'), may hold values from 0.9494358 to 13.563368
- col_stats: float32 [9216], replicated, may hold values from 1.695421 to 6.781684
- gain_stats: float32 [2, 768], P(None, 'shard'), may hold values from 0.9494358 to 13.563368
Outputs:
- text_embed: float32 [1600, 768], P(('group', 'shard'))
- image_embed: float32 [1600, 768], P(('group', 'shard'))
- grad_states: float32 [25600, 768], P(('group', 'shard'))
- weight_grad: float32 [768, 9216], P('shard')
- new_rows: float32 [4, 768], P(None, 'shard')
- new_cols: float32 [9216], replicated
- new_weights: float32 [768, 9216], P('shard')
- new_weights_low: bfloat16 [768, 9216], P('shard')
- gain_grad: float32 [2, 768], P(None, 'shard')
- new_gain_stats: float32 [2, 768], P(None, 'shard')
- new_gains: float32 [2, 768], P(None, 'shard')
- new_gains_low: bfloat16 [2, 768], P(None, 'shard')
- clip_ratios: float32 [6], replicated
The draws below stay inside these ranges and needn't reach their ends.
Inputs may be any that keep to these rules, and one draw needn't show every extreme that they name: `pair_ids`: each aligned block of 50 entries holds every number 0 to 49 once: the image of that block paired with the text.
All inputs are finite; a program needn't handle non-finite values.
Results may differ from the reference program's by a relative error of at most 0.017.
The reference program's roundings to bfloat16 on the way count: a program that leaves them out, or rounds other values in their place, can miss the bound.
Values may be sent and summed in bfloat16 or wider, within the bound.
No kernel may reach another device: no remote copies, remote signals or barrier semaphores. Data moves between devices by JAX's collectives and lax.ppermute only.
A program may use at most 256 MiB of HBM per device.

```python
import math
import jax
import jax.numpy as jnp
from jax import lax

D = 768
HEADS = 12
HEAD = 64
FF = 3072
PAIRS_DEV = 50
IMG_ROWS = 50
TXT_ROWS = 16
COLS = 9216
PAIRS = 1600


def column_scales(out_factor):
    column = jnp.arange(4 * D + 2 * FF)
    return jnp.where(column < 3 * D, D ** (-0.5), jnp.where(column < 4 * D, out_factor * D ** (-0.5), jnp.where(column < 4 * D + FF, D ** (-0.5), FF ** (-0.5))))


def falling_stats(key, count, top_ratio):
    position = jnp.arange(D, dtype=jnp.float32) / D
    jitter = jnp.exp(jax.random.uniform(key, (count, D), jnp.float32, -0.2231, 0.2231))
    level = 625.0 * PAIRS * D ** (-2.0) * jnp.exp((1.0 - position) * jnp.log(top_ratio))
    return level[None, :] * jitter


def draw_text_weights(key, part):
    key = jax.random.fold_in(key, 11)
    normal = jnp.clip(jax.random.normal(key, (D, 4 * D + 2 * FF), jnp.float32), -6.0, 6.0)
    return normal * column_scales(4.0)[None, :]


def draw_image_weights(key, part):
    key = jax.random.fold_in(key, 12)
    normal = jnp.clip(jax.random.normal(key, (D, 4 * D + 2 * FF), jnp.float32), -6.0, 6.0)
    return (normal * column_scales(5.0)[None, :]).astype(jnp.bfloat16)


def draw_text_gains(key, part):
    key = jax.random.fold_in(key, 13)
    position = jnp.arange(D, dtype=jnp.float32) / D
    jitter = jax.random.uniform(key, (2, D), jnp.float32, 0.8, 1.2)
    return (1.0 + 2.0 * position)[None, :] * jitter


def draw_pair_ids(key, part):
    key = jax.random.fold_in(key, 14)
    block_keys = jax.random.split(key, PAIRS // PAIRS_DEV)
    orders = jax.vmap(lambda block_key: jax.random.permutation(block_key, PAIRS_DEV))(block_keys)
    return orders.reshape(PAIRS).astype(jnp.int32)


def draw_row_stats(key, part):
    key = jax.random.fold_in(key, 15)
    return falling_stats(key, 4, 4.0)


def draw_gain_stats(key, part):
    key = jax.random.fold_in(key, 16)
    return falling_stats(key, 2, 4.0)


def level_of(key, shape, shards, low, high):
    def one(dim, parts):
        heights = jax.random.uniform(jax.random.fold_in(jax.random.fold_in(key, 6), dim), (parts,), jnp.float32, low / len(shards), high / len(shards))
        return jnp.repeat(jnp.exp(heights), shape[dim] // parts).reshape((-1,) + (1,) * (len(shape) - dim - 1))

    loudness = one(*shards[0])
    for cut in shards[1:]:
        loudness = loudness * one(*cut)
    return loudness


def scatter_about(rng, dims, deviation, bound, shards=(), kind=jnp.bfloat16):
    result = deviation * jax.random.normal(rng, dims, jnp.float32)
    if shards:
        result = result * level_of(rng, dims, shards, -0.22, 0.18)
    return jnp.clip(result, -bound, bound).astype(kind)


def setup_inputs(seed: int = 0) -> dict:
    splits = jax.random.split(jax.random.key(seed), 12)
    return {
        "image_states": scatter_about(splits[0], (PAIRS * IMG_ROWS, D), 1.0, 6.0, ((0, 32),)),
        "text_states": scatter_about(splits[1], (PAIRS * TXT_ROWS, D), 1.0, 6.0, ((0, 32),)),
        "image_weights": draw_image_weights(jax.random.fold_in(splits[11], 71), 0),
        "image_gains": jnp.clip(1.0 + 0.1 * jax.random.normal(splits[3], (2, D), jnp.float32), 0.5, 1.5),
        "text_weights": draw_text_weights(jax.random.fold_in(splits[11], 71), 0),
        "text_gains": draw_text_gains(jax.random.fold_in(splits[11], 71), 0),
        "logit_scale": jnp.clip(jax.random.uniform(splits[6], (), jnp.float32, 30.0, 70.0), 30.0, 70.0),
        "pair_ids": draw_pair_ids(jax.random.fold_in(splits[11], 71), 0),
        "row_stats": draw_row_stats(jax.random.fold_in(splits[11], 71), 0),
        "col_stats": jnp.clip(jnp.exp(jax.random.uniform(splits[9], (COLS,), jnp.float32, math.log(1.695421), math.log(6.781684))), 1.695421, 6.781684),
        "gain_stats": draw_gain_stats(jax.random.fold_in(splits[11], 71), 0),
    }


@jax.custom_vjp
def low(v):
    return lax.optimization_barrier(v.astype(jnp.bfloat16)).astype(jnp.float32)

@jax.custom_vjp
def low_back(v):
    return v

def low_keep(v):
    return (low(v), None)

def low_pass(kept, grad):
    return (grad,)

def back_keep(v):
    return (v, None)

def back_low(kept, grad):
    return (low(grad),)
low.defvjp(low_keep, low_pass)
low_back.defvjp(back_keep, back_low)
NORM_EPSILON = 1e-06
STAT_EPSILON = 1e-30
CLIP_LEVEL = 0.1
WEIGHT_RATE = 0.4
GAIN_RATE = 5.0

def matmul(left, right):
    return jnp.dot(left, right, precision=lax.Precision.HIGHEST, preferred_element_type=jnp.float32)

def layer_norm(value, gain_row):
    centred = value - lax.optimization_barrier(jnp.mean(value, axis=-1, keepdims=True))
    return centred * lax.rsqrt(lax.optimization_barrier(jnp.mean(centred * centred, axis=-1, keepdims=True)) + NORM_EPSILON) * gain_row

def split_weights(weights):
    return (weights[:, :3 * D], weights[:, 3 * D:4 * D], weights[:, 4 * D:4 * D + FF], weights[:, 4 * D + FF:])

def unit_rows(value):
    return value * lax.rsqrt(lax.optimization_barrier(jnp.sum(value * value, axis=-1, keepdims=True)) + NORM_EPSILON)

def image_block(states, weights, gains):
    images = states.shape[0] // IMG_ROWS
    w_qkv, w_out, w_up, w_downt = split_weights(weights)
    qkv_low = low(matmul(low(layer_norm(states, gains[0])), w_qkv)).reshape(images, IMG_ROWS, 3, HEADS, HEAD)
    scores = jnp.einsum('bhd,bkhd->bhk', qkv_low[:, 0, 0], qkv_low[:, :, 1], precision=lax.Precision.HIGHEST) * HEAD ** (-0.5)
    attn_probs = low(jax.nn.softmax(scores, axis=-1))
    mixed = jnp.einsum('bhk,bkhd->bhd', attn_probs, qkv_low[:, :, 2], precision=lax.Precision.HIGHEST).reshape(images, D)
    first = states.reshape(images, IMG_ROWS, D)[:, 0] + matmul(low(mixed), w_out)
    hidden_low = low(jax.nn.gelu(matmul(low(layer_norm(first, gains[1])), w_up)))
    return unit_rows(first + matmul(hidden_low, w_downt.T))

def text_block(states, weights, gains):
    row_count = states.shape[0]
    sequences = row_count // TXT_ROWS
    w_qkv, w_out, w_up, w_downt = split_weights(weights)
    qkv_low = low(low_back(matmul(low(layer_norm(states, gains[0])), w_qkv))).reshape(sequences, TXT_ROWS, 3, HEADS, HEAD)
    scores = low_back(jnp.einsum('bqhd,bkhd->bhqk', qkv_low[:, :, 0], qkv_low[:, :, 1], precision=lax.Precision.HIGHEST) * HEAD ** (-0.5))
    attn_probs = low(jax.nn.softmax(scores, axis=-1))
    mixed = jnp.einsum('bhqk,bkhd->bqhd', attn_probs, qkv_low[:, :, 2], precision=lax.Precision.HIGHEST).reshape(row_count, D)
    first = states + low_back(matmul(low(low_back(mixed)), w_out))
    up_value = low_back(matmul(low(layer_norm(first, gains[1])), w_up))
    return first + low_back(matmul(low(jax.nn.gelu(up_value)), w_downt.T))

def reference(image_states, text_states, image_weights, image_gains, text_weights, text_gains, logit_scale, pair_ids, row_stats, col_stats, gain_stats):
    image_rows = image_states.astype(jnp.float32).reshape(PAIRS // 64, 64 * IMG_ROWS, D)
    image_matrix = image_weights.astype(jnp.float32)
    image_embed = lax.map(lambda block_rows: image_block(block_rows, image_matrix, image_gains), image_rows).reshape(PAIRS, D)
    image_low = low(image_embed)
    target = jnp.arange(PAIRS, dtype=jnp.int32) // PAIRS_DEV * PAIRS_DEV + pair_ids

    def text_loss(states, weights, gains):
        weights_low = low(weights)
        gains_low = low(gains)
        blocks = states.reshape(PAIRS // 64, 64 * TXT_ROWS, D)
        outputs = lax.map(jax.checkpoint(lambda block_rows: text_block(block_rows, weights_low, gains_low)), blocks)
        pooled = lax.optimization_barrier(jnp.mean(outputs.reshape(PAIRS, TXT_ROWS, D), axis=1))
        text_embed = unit_rows(pooled)
        cosine = low_back(matmul(low(text_embed), image_low.T))
        scores = logit_scale * cosine
        positive = jnp.sum(jnp.take_along_axis(scores, target[:, None], axis=1))
        loss_value = 0.5 * (jnp.sum(jax.nn.logsumexp(scores, axis=1)) + jnp.sum(jax.nn.logsumexp(scores, axis=0))) - positive
        return (loss_value, text_embed)
    loss_value, pullback, text_embed = jax.vjp(text_loss, text_states.astype(jnp.float32), text_weights, text_gains, has_aux=True)
    grad_states, weight_grad, gain_grad = pullback(jnp.ones((), jnp.float32))
    bounds = (0, 3 * D, 4 * D, 4 * D + FF, 4 * D + 2 * FF)
    squares = weight_grad * weight_grad + STAT_EPSILON
    new_rows = 0.5 * row_stats + 0.5 * jnp.stack([lax.optimization_barrier(jnp.mean(squares[:, bounds[which]:bounds[which + 1]], axis=1)) for which in range(4)])
    new_cols = 0.5 * col_stats + 0.5 * lax.optimization_barrier(jnp.mean(squares, axis=0))
    segments = []
    ratio_list = []
    for which in range(4):
        lower, upper = (bounds[which], bounds[which + 1])
        estimate = new_rows[which][:, None] * new_cols[lower:upper][None, :] / jnp.mean(new_rows[which])
        segment = weight_grad[:, lower:upper] * lax.rsqrt(estimate)
        clip_ratio = jnp.maximum(1.0, jnp.sqrt(jnp.mean(segment * segment)) / CLIP_LEVEL)
        ratio_list.append(clip_ratio)
        segments.append(segment / clip_ratio)
    new_weights = text_weights - WEIGHT_RATE * jnp.concatenate(segments, axis=1)
    new_gain_stats = 0.5 * gain_stats + 0.5 * (gain_grad * gain_grad + STAT_EPSILON)
    gain_update = gain_grad * lax.rsqrt(new_gain_stats)
    gain_ratio = jnp.maximum(1.0, jnp.sqrt(lax.optimization_barrier(jnp.mean(gain_update * gain_update, axis=1))) / CLIP_LEVEL)
    new_gains = text_gains - GAIN_RATE * gain_update / gain_ratio[:, None]
    clip_ratios = jnp.concatenate([jnp.stack(ratio_list), gain_ratio])
    return (text_embed, image_embed, grad_states, weight_grad, new_rows, new_cols, new_weights, new_weights.astype(jnp.bfloat16), gain_grad, new_gain_stats, new_gains, new_gains.astype(jnp.bfloat16), clip_ratios)
```

```python
import functools

import jax
import jax.numpy as jnp
import numpy as np
from jax import lax
from jax.experimental import pallas as pl
from jax.experimental.pallas import tpu as pltpu
from jax.sharding import PartitionSpec as P

HEADS = 12
IMG_ROWS = 50
TXT_ROWS = 16
NORM_EPSILON = 1e-06
STAT_EPSILON = 1e-30
CLIP_LEVEL = 0.1
WEIGHT_RATE = 0.4
GAIN_RATE = 5.0
GELU_SCALE = 0.7978845608028654
GELU_CUBE = 0.044715
MASKED = -1e30
IMAGES_STEP = 8
FF_STEPS = 4
ROW_STEPS = 2
TEXTS_GROUP = 5
VMEM_LIMIT = 24 * 1024 * 1024
VMEM_MORE = 48 * 1024 * 1024
VMEM_MOST = 62 * 1024 * 1024
COST_SCALE = 100


def to_low(value):
    return value.astype(jnp.bfloat16)


def wide(value):
    return value.astype(jnp.float32)


def dot(left, right):
    return jnp.dot(left, right, preferred_element_type=jnp.float32)


def dot_tn(left, right):
    return lax.dot_general(
        left, right, (((0,), (0,)), ((), ())), preferred_element_type=jnp.float32
    )


def dot_nt(left, right):
    return lax.dot_general(
        left, right, (((1,), (1,)), ((), ())), preferred_element_type=jnp.float32
    )


def iota(shape, axis):
    return lax.broadcasted_iota(jnp.int32, shape, axis)


def normalize(value):
    centred = value - jnp.mean(value, axis=-1, keepdims=True)
    inverse = lax.rsqrt(jnp.mean(centred * centred, axis=-1, keepdims=True) + NORM_EPSILON)
    return (centred * inverse, inverse)


def norm_back(grad_hat, normed, inverse):
    return inverse * (
        grad_hat
        - jnp.mean(grad_hat, axis=-1, keepdims=True)
        - normed * jnp.mean(grad_hat * normed, axis=-1, keepdims=True)
    )


def gelu(value):
    bent = jnp.tanh(GELU_SCALE * (value + GELU_CUBE * value * value * value))
    return 0.5 * value * (1.0 + bent)


def gelu_slope(value):
    inner = GELU_SCALE + (GELU_SCALE * GELU_CUBE) * (value * value)
    share = 0.5 + 0.5 * jnp.tanh(value * inner)
    result = value * share
    slope = share + (result - result * share) * (6.0 * inner - 4.0 * GELU_SCALE)
    return result, slope


def blocks_of(total, size=32):
    return [slice(start, min(start + size, total)) for start in range(0, total, size)]


def halves_mask(rows, width):
    lane = iota((rows, width), 1)
    return to_low((lane < width // 2).astype(jnp.float32))


def call(kernel, grid, in_specs, out_specs, out_shapes, scratch, args, flops, after=(), place=None, least=2e9, vmem=VMEM_LIMIT, large=()):
    moved = sum(a.size * a.dtype.itemsize for a in args)
    moved += sum(o.size * o.dtype.itemsize for o in out_shapes)
    lead = 0 if place is None else 1
    body = kernel
    if after:
        first, skipped = lead + len(args), len(after)

        def body(*refs):
            kernel(*refs[:first], *refs[first + skipped :])

    in_specs = list(in_specs) + [pl.BlockSpec(memory_space=pl.ANY)] * len(after)
    spec = dict(grid=grid, in_specs=in_specs, out_specs=out_specs, scratch_shapes=scratch)
    if place is not None:
        spec = dict(
            grid_spec=pltpu.PrefetchScalarGridSpec(num_scalar_prefetch=1, **spec)
        )
        args = (place,) + tuple(args)
    out_shapes = [
        pltpu.MemorySpace.HBM(out.shape, out.dtype) if index in large else out
        for index, out in enumerate(out_shapes)
    ]
    return pl.pallas_call(
        body,
        out_shape=out_shapes,
        compiler_params=pltpu.CompilerParams(vmem_limit_bytes=vmem),
        cost_estimate=pl.CostEstimate(
            flops=int(COST_SCALE * max(flops, least)),
            bytes_accessed=int(COST_SCALE * moved),
            transcendentals=0,
        ),
        **spec,
    )(*args, *after)


def room(images):
    return VMEM_LIMIT if images * 2 < VMEM_LIMIT // 2 else VMEM_MOST


def shape(dims, dtype=jnp.float32):
    return jax.ShapeDtypeStruct(dims, dtype)


def whole(array):
    zeros = (0,) * array.ndim
    return pl.BlockSpec(array.shape, lambda *_: zeros)


def some(array, first, count):
    return pl.BlockSpec(
        (count,) + array.shape[1:], lambda *_: (first // count,) + (0,) * (array.ndim - 1)
    )


SMEM = pl.BlockSpec(memory_space=pltpu.SMEM)


def image_attention_kernel(
    total_rows,
    x_ref, wq_ref, wk_ref, wv_ref, wo_ref, gain_ref,
    out_ref,
    rows_scr, x_scr, class_scr, query_scr, mixed_scr, low_scr,
):
    phase, step = pl.program_id(0), pl.program_id(1)
    steps = pl.num_programs(1)
    count, rows, width = rows_scr.shape
    images = IMAGES_STEP
    pairs = HEADS // 2
    pair = width // pairs

    @pl.when(phase == 0)
    def _():
        x = wide(x_ref[...])
        x = jnp.where(step * rows + iota((rows, 1), 0) < total_rows, x, 0.0)
        a = to_low(normalize(x)[0] * gain_ref[0:1, :])
        rows_scr[step] = a
        pick = iota((images, rows), 1) == iota((images, rows), 0) * IMG_ROWS
        pick = to_low(pick.astype(jnp.float32))
        class_scr[step] = dot(pick, a)
        x_scr[step] = dot(pick, to_low(x))

    @pl.when((phase == 1) & (step == 0))
    def _():
        query = to_low(dot(to_low(class_scr[...].reshape(count * images, width)), wq_ref[...]))
        first = halves_mask(count * images, pair)
        for which in range(pairs):
            lanes = slice(which * pair, (which + 1) * pair)
            for half in range(2):
                head = 2 * which + half
                own = query[:, lanes] * (first if half == 0 else 1 - first)
                query_scr[:, head * images : (head + 1) * images, :] = dot_nt(
                    own, wk_ref[:, lanes]
                ).reshape(count, images, width)

    @pl.when(phase == 1)
    def _():
        a = rows_scr[step]
        scores = dot_nt(to_low(query_scr[step]), a) * (width // HEADS) ** (-0.5)
        start = (iota(scores.shape, 0) & (images - 1)) * IMG_ROWS
        column = iota(scores.shape, 1)
        scores = jnp.where((column >= start) & (column < start + IMG_ROWS), scores, MASKED)
        power = jnp.exp(scores - jnp.max(scores, axis=-1, keepdims=True))
        probs = power / jnp.sum(power, axis=-1, keepdims=True)
        mixed_scr[step] = dot(to_low(probs), a)

    @pl.when((phase == 1) & (step == steps - 1))
    def _():
        lane = iota((count * images, pair), 1)
        for which in range(pairs):
            lanes = slice(which * pair, (which + 1) * pair)
            halves = []
            for half in range(2):
                head = 2 * which + half
                own = mixed_scr[:, head * images : (head + 1) * images, :]
                halves.append(dot(to_low(own.reshape(count * images, width)), wv_ref[:, lanes]))
            low_scr[:, lanes] = to_low(jnp.where(lane < pair // 2, halves[0], halves[1]))
        out_ref[...] = x_scr[...].reshape(count * images, width) + dot(low_scr[...], wo_ref[...])


def image_attention(states, weights, gains, after=()):
    total_rows, width = states.shape
    rows = IMAGES_STEP * IMG_ROWS
    steps = pl.cdiv(total_rows, rows)
    padded = steps * IMAGES_STEP

    def part(which):
        return pl.BlockSpec((width, width), lambda phase, step: (0, which))

    return call(
        functools.partial(image_attention_kernel, total_rows),
        (2, steps),
        [
            pl.BlockSpec(
                (rows, width), lambda phase, step: (jnp.where(phase == 0, step, steps - 1), 0)
            ),
            part(0), part(1), part(2), part(3),
            whole(gains),
        ],
        [pl.BlockSpec((padded, width), lambda phase, step: (0, 0))],
        [shape((padded, width))],
        [
            pltpu.VMEM((steps, rows, width), jnp.bfloat16),
            pltpu.VMEM((steps, IMAGES_STEP, width), jnp.float32),
            pltpu.VMEM((steps, IMAGES_STEP, width), jnp.float32),
            pltpu.VMEM((steps, HEADS * IMAGES_STEP, width), jnp.float32),
            pltpu.VMEM((steps, HEADS * IMAGES_STEP, width), jnp.float32),
            pltpu.VMEM((padded, width), jnp.bfloat16),
        ],
        (states, weights, weights, weights, weights, gains),
        4 * total_rows * width * HEADS * IMAGES_STEP * 3,
        after,
        vmem=VMEM_MORE,
    )[0]


def image_mlp_kernel(x_ref, gain_ref, up_ref, down_ref, out_ref, low_ref, norm_scr, total_scr):
    step = pl.program_id(0)

    @pl.when(step == 0)
    def _():
        norm_scr[...] = to_low(normalize(x_ref[...])[0] * gain_ref[1:2, :])
        total_scr[...] = x_ref[...]

    hidden = to_low(gelu(dot(norm_scr[...], up_ref[...])))
    total_scr[...] += dot_nt(hidden, down_ref[...])

    @pl.when(step == pl.num_programs(0) - 1)
    def _():
        result = total_scr[...]
        result = result * lax.rsqrt(
            jnp.sum(result * result, axis=-1, keepdims=True) + NORM_EPSILON
        )
        count = out_ref.shape[0]
        out_ref[...] = result[:count]
        low_ref[...] = jnp.zeros_like(low_ref)
        low_ref[: result.shape[0], :] = to_low(
            jnp.where(iota(result.shape, 0) < count, result, 0.0)
        )


def image_mlp(first, weights, gains, images, after=()):
    padded, width = first.shape
    hidden = (weights.shape[1] - 4 * width) // 2
    block = hidden // FF_STEPS
    lead = 4 * width // block
    return call(
        image_mlp_kernel,
        (FF_STEPS,),
        [
            whole(first),
            whole(gains),
            pl.BlockSpec((width, block), lambda step: (0, lead + step)),
            pl.BlockSpec((width, block), lambda step: (0, lead + FF_STEPS + step)),
        ],
        [
            pl.BlockSpec((images, width), lambda step: (0, 0)),
            pl.BlockSpec((pair_rows(padded), width), lambda step: (0, 0)),
        ],
        [shape((images, width)), shape((pair_rows(padded), width), jnp.bfloat16)],
        [pltpu.VMEM((padded, width), jnp.bfloat16), pltpu.VMEM((padded, width), jnp.float32)],
        (first, gains, weights, weights),
        4 * padded * width * hidden * 3,
        after,
        vmem=VMEM_MORE,
    )


class Place:
    def __init__(self, chips, rows, groups, stacked=False, halves=False):
        self.chips, self.rows, self.groups = chips, rows, groups
        self.stacked, self.halves = stacked, halves

    def column(self, step, group):
        if not self.halves:
            return step ^ group
        side = step & 1
        return 2 * side + (((group >> side) & 1) ^ (step >> 1))


def weight_copies(place, pos_ref, blocks, w_scr, sems):
    if place is None:
        return [[pltpu.make_async_copy(blocks[0], w_scr, sems.at[0])]]
    copies = [[] for _ in range(place.groups)]
    width = w_scr.shape[2] // place.groups
    count = 0
    for ref, lines, masks, same_core in blocks:
        for index, (line, mask) in enumerate((l, m) for m in masks for l in lines):
            core = pos_ref[1] if same_core else 1 - pos_ref[1]
            row = (pos_ref[0] ^ line) * 2 + core
            if place.stacked:
                target = w_scr.at[row * place.groups + (pos_ref[2] ^ mask)]
            else:
                column = pl.multiple_of(place.column(mask, pos_ref[2]) * width, width)
                target = w_scr.at[row, :, pl.ds(column, width)]
            copies[mask].append(pltpu.make_async_copy(ref.at[index], target, sems.at[count]))
            count += 1
    return copies


def load_weights(copies, step):
    @pl.when(step == 0)
    def _():
        for group in copies:
            for copy in group:
                copy.start()

    for mask, group in enumerate(copies):

        @pl.when(step == mask)
        def _():
            for copy in group:
                copy.wait()


class Weights:
    def __init__(self, place, arrays, keys, columns):
        self.place, self.arrays, self.keys, self.columns = place, arrays, keys, columns

    def specs(self):
        return [pl.BlockSpec(memory_space=pl.ANY)] * len(self.arrays)

    def blocks(self, refs):
        if self.place is None:
            return list(refs)
        return [(ref,) + key for ref, key in zip(refs, self.keys)]

    def scratch(self, width):
        if self.place is None:
            dims, count = self.arrays[0].shape, 1
        else:
            count = 2 * self.place.chips * self.place.groups
            shards = count if self.place.stacked else 2 * self.place.chips
            dims = (shards, self.place.rows, self.columns)
        return [pltpu.VMEM(dims, jnp.bfloat16), pltpu.SemaphoreType.DMA((count,))]

    def column(self, step, group):
        return step if self.place is None else self.place.column(step, group)

    def lanes(self, pos_ref, step, block):
        return pl.ds(pl.multiple_of(self.column(step, pos_ref[2]) * block, block), block)

    def out(self, width):
        return jax.ShapeDtypeStruct(self.scratch(width)[0].shape, jnp.bfloat16)


def rows_of(ref, lanes):
    value = ref[:, :, lanes]
    return value.reshape(value.shape[0] * value.shape[1], value.shape[2])


GROUP = 4 * TXT_ROWS


def group_bias(width):
    key = lax.shift_right_logical(iota((GROUP, width), 0), 4)
    query = lax.shift_right_logical(iota((GROUP, width), 1) & (GROUP - 1), 4)
    return jnp.where(key == query, 0.0, MASKED)


def group_softmax(scores, bias):
    scores = scores + bias
    power = jnp.exp(scores - jnp.max(scores, axis=0, keepdims=True))
    return power * (1.0 / jnp.sum(power, axis=0, keepdims=True))


def both_heads(value, first, second):
    return jnp.concatenate([value * first, value * second], axis=0)


def group_rows(rows):
    for start in range(0, rows, GROUP):
        start = min(start, rows - GROUP)
        yield slice(start, start + GROUP)


def project_kernel(weights, count, pos_ref, x_ref, gain_ref, *refs):
    block_refs, refs = refs[:count], refs[count:]
    qkv_ref, w_out_ref, norm_scr, w_scr, sems, out_sem = refs
    width = x_ref.shape[1]
    step = pl.program_id(0)
    copies = weight_copies(weights.place, pos_ref, weights.blocks(block_refs), w_scr, sems)
    copy_out = pltpu.make_async_copy(w_scr, w_out_ref, out_sem)
    load_weights(copies, step)

    @pl.when(step == 0)
    def _():
        norm_scr[...] = to_low(normalize(wide(x_ref[...]))[0] * gain_ref[0:1, :])

    @pl.when(step == pl.num_programs(0) - 1)
    def _():
        copy_out.start()

    @pl.when(weights.column(step, pos_ref[2]) < 3)
    def _():
        w = rows_of(w_scr, weights.lanes(pos_ref, step, width))
        products = [dot(norm_scr[...], w[:, lanes]) for lanes in blocks_of(width, COLUMN_CHUNK)]
        for lanes, product in zip(blocks_of(width, COLUMN_CHUNK), products):
            qkv_ref[:, lanes] = to_low(product)

    @pl.when(step == pl.num_programs(0) - 1)
    def _():
        copy_out.wait()


def project(states, weights, gains, pos, after=()):
    total, width = states.shape
    qkv, full = call(
        functools.partial(project_kernel, weights, len(weights.arrays)),
        (4,),
        [whole(states), whole(gains)] + weights.specs(),
        [
            pl.BlockSpec((total, width), lambda step, pos: (0, weights.column(step, pos[2]))),
            pl.BlockSpec(memory_space=pl.ANY),
        ],
        [shape((total, 4 * width), jnp.bfloat16), weights.out(width)],
        [pltpu.VMEM((total, width), jnp.bfloat16)]
        + weights.scratch(width)
        + [pltpu.SemaphoreType.DMA],
        (states, gains, *weights.arrays),
        6 * total * width * width * 1.5,
        after,
        pos,
        large=(1,),
    )
    return qkv, full.reshape(width, -1)


def attention_forward_kernel(x_ref, qkv_ref, w_ref, mixed_ref, out_ref):
    rows, width = x_ref.shape
    pairs = HEADS // 2
    pair = width // pairs
    scale = (width // HEADS) ** (-0.5)
    first = halves_mask(GROUP, pair)
    second = 1 - first
    first_scaled, second_scaled = first * scale, second * scale
    bias = group_bias(width)
    lane = iota((GROUP, pair), 1)

    def part(here, which, kind):
        start = kind * width + which * pair
        return qkv_ref[here, start : start + pair]

    def scores_of(here):
        scores = [
            dot_nt(
                part(here, which, 1), both_heads(part(here, which, 0), first_scaled, second_scaled)
            )
            for which in range(pairs)
        ]
        return jnp.concatenate(scores, axis=1)

    groups = list(group_rows(rows))
    scores = scores_of(groups[0])
    for index, here in enumerate(groups):
        following = scores_of(groups[index + 1]) if index + 1 < len(groups) else None
        probs = to_low(group_softmax(scores, bias))
        both = [
            dot_tn(probs[:, which * pair : (which + 1) * pair], part(here, which, 2))
            for which in range(pairs)
        ]
        for which in range(pairs):
            mixed_ref[here, which * pair : (which + 1) * pair] = to_low(
                jnp.where(lane < pair // 2, both[which][:GROUP], both[which][GROUP:])
            )
        scores = following
    out_ref[...] = wide(x_ref[...]) + dot(mixed_ref[...], w_ref[...])


def attention_forward(states, qkv, weights, after=()):
    total, width = states.shape
    rows = total // ROW_STEPS

    def by_rows(columns):
        return pl.BlockSpec((rows, columns), lambda step: (step, 0))

    return call(
        attention_forward_kernel,
        (ROW_STEPS,),
        [by_rows(width), by_rows(3 * width), pl.BlockSpec((width, width), lambda step: (0, 3))],
        [by_rows(width), by_rows(width)],
        [shape((total, width), jnp.bfloat16), shape((total, width))],
        [],
        (states, qkv, weights),
        6 * total * width * width * 1.5,
        after,
    )


def split_low(value):
    high = to_low(value)
    return high, to_low(value - wide(high))


def pair_rows(texts):
    return -(-texts // 16) * 16


def store_pair(ref, texts, high, low):
    half = pair_rows(texts)
    ref[...] = jnp.zeros_like(ref)
    ref[:texts, :] = high
    ref[half : half + texts, :] = low


COLUMN_CHUNK = 256


def up_kernel(weights, count, pos_ref, x_ref, gain_ref, *refs):
    block_refs, refs = refs[:count], refs[count:]
    hidden_ref, slope_ref, pooled_ref, w_out_ref, norm_scr, low_scr, w_scr, sems, out_sem = refs
    total, width = x_ref.shape
    texts = total // TXT_ROWS
    block = hidden_ref.shape[1]
    step = pl.program_id(0)
    last = pl.num_programs(0) - 1
    copies = weight_copies(weights.place, pos_ref, weights.blocks(block_refs), w_scr, sems)
    copy_out = pltpu.make_async_copy(w_scr, w_out_ref, out_sem)
    load_weights(copies, step)

    @pl.when(step == 0)
    def _():
        x = x_ref[...]
        norm_scr[...] = to_low(normalize(x)[0] * gain_ref[1:2, :])
        pooled_ref[...] = jnp.sum(x.reshape(texts, TXT_ROWS, width), axis=1)

    @pl.when(step == last)
    def _():
        copy_out.start()

    w = rows_of(w_scr, weights.lanes(pos_ref, step, block))
    pool = lax.shift_right_logical(iota((texts, total), 1), 4) == iota((texts, total), 0)
    pool = to_low(pool.astype(jnp.float32))
    chunks = blocks_of(block, COLUMN_CHUNK)
    product = dot(norm_scr[...], w[:, chunks[0]])
    for index, lanes in enumerate(chunks):
        following = None
        if index + 1 < len(chunks):
            following = dot(norm_scr[...], w[:, chunks[index + 1]])
        value, slope = gelu_slope(product)
        slope_ref[:, lanes] = to_low(slope)
        low_scr[:, lanes] = to_low(value)
        product = following
    store_pair(hidden_ref, texts, *split_low(dot(pool, low_scr[...])))

    @pl.when(step == last)
    def _():
        copy_out.wait()


def up_forward(states, weights, gains, pos, after=()):
    total, width = states.shape
    hidden = weights.columns
    block = hidden // FF_STEPS
    texts = total // TXT_ROWS
    columns = lambda step, pos: (0, weights.column(step, pos[2]))
    hidden_sum, slope, pooled, full = call(
        functools.partial(up_kernel, weights, len(weights.arrays)),
        (FF_STEPS,),
        [whole(states), whole(gains)] + weights.specs(),
        [
            pl.BlockSpec((2 * pair_rows(texts), block), columns),
            pl.BlockSpec((total, block), columns),
            pl.BlockSpec((texts, width), lambda step, pos: (0, 0)),
            pl.BlockSpec(memory_space=pl.ANY),
        ],
        [
            shape((2 * pair_rows(texts), hidden), jnp.bfloat16),
            shape((total, hidden), jnp.bfloat16), shape((texts, width)),
            weights.out(width),
        ],
        [pltpu.VMEM((total, width), jnp.bfloat16), pltpu.VMEM((total, block), jnp.bfloat16)]
        + weights.scratch(width)
        + [pltpu.SemaphoreType.DMA],
        (states, gains, *weights.arrays),
        2 * total * width * hidden * 1.5,
        after,
        pos,
        large=(1, 3),
    )
    return hidden_sum, slope, pooled, full.reshape(width, -1)


def scores_kernel(
    weights, count, images, image_count, pos_ref,
    hidden_ref, pooled_ref, bias_ref, scale_ref, *refs,
):
    block_refs, refs = refs[:count], refs[count:]
    image_refs, refs = refs[:image_count], refs[image_count:]
    embed_ref, inverse_ref, scores_ref, row_ref, col_ref, w_out_ref, image_out_ref = refs[:7]
    total_scr, w_scr, sems, out_sem, image_scr, image_sems, image_out_sem = refs[7:]
    step = pl.program_id(0)
    last = pl.num_programs(0) - 1
    texts = embed_ref.shape[0]
    half = pair_rows(texts)
    copies = weight_copies(weights.place, pos_ref, weights.blocks(block_refs), w_scr, sems)
    copy_out = pltpu.make_async_copy(w_scr, w_out_ref, out_sem)
    image_copies = weight_copies(
        images.place, pos_ref, images.blocks(image_refs), image_scr, image_sems
    )
    image_out = pltpu.make_async_copy(image_scr, image_out_ref, image_out_sem)
    load_weights(copies, step)

    @pl.when(step == 0)
    def _():
        total_scr[...] = pooled_ref[...]
        for group in image_copies:
            for copy in group:
                copy.start()

    @pl.when(step == last)
    def _():
        copy_out.start()

    w = rows_of(w_scr, weights.lanes(pos_ref, step, hidden_ref.shape[1]))
    both = dot_nt(hidden_ref[...], w)
    total_scr[...] += both[:texts] + both[half : half + texts]

    @pl.when(step == last)
    def _():
        for group in image_copies:
            for copy in group:
                copy.wait()
        image_out.start()
        pooled = total_scr[...] * (1.0 / TXT_ROWS)
        inverse = lax.rsqrt(jnp.sum(pooled * pooled, axis=-1, keepdims=True) + NORM_EPSILON)
        embed = pooled * inverse
        embed_ref[...] = embed
        inverse_ref[...] = inverse
        all_image = rows_of(image_scr, slice(0, image_scr.shape[2]))
        scores = scale_ref[0, 0] * dot_nt(to_low(embed), all_image) + bias_ref[...]
        scores_ref[...] = scores
        top = jnp.max(scores, axis=1, keepdims=True)
        row_ref[...] = top + jnp.log(jnp.sum(jnp.exp(scores - top), axis=1, keepdims=True))
        top = jnp.max(scores, axis=0, keepdims=True)
        col_ref[...] = top + jnp.log(jnp.sum(jnp.exp(scores - top), axis=0, keepdims=True))
        copy_out.wait()
        image_out.wait()


def scores_forward(hidden, pooled, weights, images, bias, scale, pos, after=()):
    texts, width = pooled.shape
    total = hidden.shape[1]
    block = total // FF_STEPS
    count = bias.shape[1]
    outs = [
        shape((texts, width)), shape((texts, 1)), shape((texts, count)),
        shape((texts, 1)), shape((1, count)),
    ]
    *results, full, full_images = call(
        functools.partial(
            scores_kernel, weights, len(weights.arrays), images, len(images.arrays)
        ),
        (FF_STEPS,),
        [
            pl.BlockSpec(
                (hidden.shape[0], block), lambda step, pos: (0, weights.column(step, pos[2]))
            ),
            whole(pooled), whole(bias), SMEM,
        ]
        + weights.specs()
        + images.specs(),
        [whole(out) for out in outs] + [pl.BlockSpec(memory_space=pl.ANY)] * 2,
        outs + [weights.out(width), images.out(width)],
        [pltpu.VMEM((texts, width), jnp.float32)]
        + weights.scratch(width)
        + [pltpu.SemaphoreType.DMA]
        + images.scratch(width)
        + [pltpu.SemaphoreType.DMA],
        (hidden, pooled, bias, scale, *weights.arrays, *images.arrays),
        2 * texts * width * (2 * total + count) * 3,
        after,
        pos,
        vmem=room(count * width),
        large=(5, 6),
    )
    return *results, full.reshape(width, -1), full_images.reshape(count, width)


class Split:
    def __init__(self, place, width, columns, lines_first=False):
        self.place, self.width, self.columns = place, width, columns
        self.lines_first = lines_first

    def specs(self):
        if self.place is None:
            return [pl.BlockSpec((self.width, self.columns), lambda step, pos: (0, step))]
        tail = (self.place.rows, self.columns)
        if self.lines_first:
            block = (self.place.chips, 1) + tail
            return [pl.BlockSpec(block, lambda step, pos: (0, step ^ pos[2], 0, 0))] * 2
        block = (1, self.place.chips) + tail
        return [pl.BlockSpec(block, lambda step, pos: (step ^ pos[2], 0, 0, 0))] * 2

    def outs(self, steps):
        if self.place is None:
            return [shape((self.width, steps * self.columns), jnp.bfloat16)]
        lead = (self.place.chips, steps) if self.lines_first else (steps, self.place.chips)
        return [shape(lead + (self.place.rows, self.columns), jnp.bfloat16)] * 2

    def scratch(self):
        if self.place is None:
            return []
        return [
            pltpu.VMEM((2 * self.place.chips, self.place.rows, self.columns), jnp.bfloat16)
        ]

    def store(self, value, refs, scr, pos_ref):
        if self.place is None:
            refs[0][...] = to_low(value)
            return
        scr[0][...] = to_low(value).reshape(scr[0].shape)
        for line in range(self.place.chips):
            row = (pos_ref[0] ^ line) * 2
            at = (line, 0) if self.lines_first else (0, line)
            refs[0][at] = scr[0][row + pos_ref[1]]
            refs[1][at] = scr[0][row + 1 - pos_ref[1]]


def scores_backward_kernel(
    split, pos_ref,
    scores_ref, row_ref, col_ref, target_ref, scale_ref, image_ref, embed_ref, inverse_ref,
    hidden_ref, w_ref,
    grad_hidden_ref, grad_out_ref, *refs,
):
    count = len(split.specs())
    grad_refs, low_scr, scr = refs[:count], refs[count], refs[count + 1 :]

    @pl.when(pl.program_id(0) == 0)
    def _():
        scores = scores_ref[...]
        hit = (iota(scores.shape, 1) == target_ref[...]).astype(jnp.float32)
        grad = scale_ref[0, 0] * (
            0.5 * (jnp.exp(scores - row_ref[...]) + jnp.exp(scores - col_ref[...])) - hit
        )
        grad_text = dot(to_low(grad), image_ref[...])
        embed = embed_ref[...]
        grad_pooled = inverse_ref[...] * (
            grad_text - embed * jnp.sum(embed * grad_text, axis=-1, keepdims=True)
        )
        grad_out = grad_pooled * (1.0 / TXT_ROWS)
        grad_out_ref[...] = grad_out
        store_pair(low_scr, grad_out.shape[0], to_low(grad_out), to_low(grad_out))

    branch = low_scr[...]
    grad_hidden_ref[...] = dot(branch[: grad_hidden_ref.shape[0]], w_ref[...])
    split.store(dot_tn(branch, hidden_ref[...]), grad_refs, scr, pos_ref)


def scores_backward(
    scores, row, col, target, scale, images, embed, inverse, hidden, weights, place, pos, after=()
):
    texts, width = embed.shape
    total = hidden.shape[1]
    block = total // FF_STEPS
    split = Split(place, width, block)
    columns = lambda step, pos: (0, step)
    grad_hidden, grad_out, *grads = call(
        functools.partial(scores_backward_kernel, split),
        (FF_STEPS,),
        [
            whole(scores), whole(row), whole(col), whole(target), SMEM, whole(images),
            whole(embed), whole(inverse),
            pl.BlockSpec((hidden.shape[0], block), columns),
            pl.BlockSpec((width, block), columns),
        ],
        [
            pl.BlockSpec((texts, block), columns),
            pl.BlockSpec((texts, width), lambda step, pos: (0, 0)),
        ]
        + split.specs(),
        [shape((texts, total)), shape((texts, width))] + split.outs(FF_STEPS),
        [pltpu.VMEM((hidden.shape[0], width), jnp.bfloat16)] + split.scratch(),
        (scores, row, col, target, scale, images, embed, inverse, hidden, weights),
        2 * texts * width * (3 * total + scores.shape[1]) * 3,
        after,
        pos,
        vmem=room(images.size),
        large=(2, 3),
    )
    return grad_hidden, grad_out, grads


def turned_norm_kernel(which, x_ref, gain_ref, out_ref):
    out_ref[...] = to_low(normalize(wide(x_ref[...]))[0] * gain_ref[which : which + 1, :]).T


def turned_norm(states, gains, which, after=()):
    total, width = states.shape
    return call(
        functools.partial(turned_norm_kernel, which),
        (1,),
        [whole(states), whole(gains)],
        [pl.BlockSpec((width, total), lambda step: (0, 0))],
        [shape((width, total), jnp.bfloat16)],
        [],
        (states, gains),
        10 * total * width,
        after,
    )[0]


def up_backward_kernel(split, pos_ref, grad_ref, slope_ref, norm_ref, w_ref, grad_x_ref, *refs):
    count = len(split.specs())
    grad_refs, scr = refs[:count], refs[count:]
    texts, block = grad_ref.shape
    total = slope_ref.shape[0]

    @pl.when(pl.program_id(0) == 0)
    def _():
        grad_x_ref[...] = jnp.zeros_like(grad_x_ref)

    spread = jnp.broadcast_to(grad_ref[...][:, None, :], (texts, TXT_ROWS, block))
    grad = to_low(spread.reshape(total, block) * wide(slope_ref[...]))
    grad_w = dot(norm_ref[...], grad)
    grad_x = dot_nt(grad, w_ref[...])
    split.store(grad_w, grad_refs, scr, pos_ref)
    grad_x_ref[...] += grad_x


def up_backward(grad_hidden, slope, norm, weights, place, pos, after=()):
    width, total = norm.shape
    texts, hidden = grad_hidden.shape
    block = hidden // FF_STEPS
    split = Split(place, width, block)
    columns = lambda step, pos: (0, step)
    grad_x, *grads = call(
        functools.partial(up_backward_kernel, split),
        (FF_STEPS,),
        [
            pl.BlockSpec((texts, block), columns),
            pl.BlockSpec((total, block), columns),
            whole(norm),
            pl.BlockSpec((width, block), columns),
        ],
        [pl.BlockSpec((total, width), lambda step, pos: (0, 0))] + split.specs(),
        [shape((total, width))] + split.outs(FF_STEPS),
        split.scratch(),
        (grad_hidden, slope, norm, weights),
        4 * total * width * hidden * 1.5,
        after,
        pos,
        large=(1, 2),
    )
    return grad_x, grads


def first_backward_kernel(
    grad_b_ref, grad_out_ref, x_ref, gain_ref, w_ref,
    grad_x_ref, grad_low_ref, grad_mixed_ref, grad_gain_ref,
):
    rows, width = x_ref.shape
    texts = rows // TXT_ROWS
    hat, inverse = normalize(x_ref[...])
    grad_b = grad_b_ref[...]
    grad_gain = jnp.sum(grad_b * hat, axis=0, keepdims=True)
    spread = jnp.broadcast_to(grad_out_ref[...].reshape(texts, 1, width), (texts, TXT_ROWS, width))
    grad_x = spread.reshape(rows, width) + norm_back(grad_b * gain_ref[1:2, :], hat, inverse)
    grad_x_ref[...] = grad_x
    grad_low = to_low(grad_x)
    grad_low_ref[...] = grad_low
    grad_mixed_ref[...] = to_low(dot_nt(grad_low, w_ref[...]))

    @pl.when(pl.program_id(0) == 0)
    def _():
        grad_gain_ref[...] = grad_gain

    @pl.when(pl.program_id(0) > 0)
    def _():
        grad_gain_ref[...] += grad_gain


def first_backward(grad_b, grad_out, states, gains, weights, after=()):
    total, width = states.shape
    rows = total // ROW_STEPS
    texts = rows // TXT_ROWS
    by_rows = pl.BlockSpec((rows, width), lambda step: (step, 0))
    return call(
        first_backward_kernel,
        (ROW_STEPS,),
        [
            by_rows,
            pl.BlockSpec((1, texts, width), lambda step: (step, 0, 0)),
            by_rows,
            whole(gains),
            pl.BlockSpec((width, width), lambda step: (0, 3)),
        ],
        [by_rows, by_rows, by_rows, pl.BlockSpec((1, width), lambda step: (0, 0))],
        [
            shape((total, width)),
            shape((total, width), jnp.bfloat16),
            shape((total, width), jnp.bfloat16),
            shape((1, width)),
        ],
        [],
        (grad_b, grad_out.reshape(ROW_STEPS, texts, width), states, gains, weights),
        2 * total * width * width * 1.5,
        after,
    )


def attention_backward_kernel(qkv_ref, grad_ref, grad_qkv_ref):
    rows, width = grad_ref.shape
    pairs = HEADS // 2
    pair = width // pairs
    scale = (width // HEADS) ** (-0.5)
    first = halves_mask(GROUP, pair)
    second = 1 - first
    first_scaled, second_scaled = first * scale, second * scale
    bias = group_bias(width)
    lane = iota((GROUP, pair), 1)

    def part(here, which, kind):
        start = kind * width + which * pair
        return qkv_ref[here, start : start + pair]

    def products_of(here):
        queries = [
            both_heads(part(here, which, 0), first_scaled, second_scaled) for which in range(pairs)
        ]
        grads = [
            both_heads(grad_ref[here, which * pair : (which + 1) * pair], first, second)
            for which in range(pairs)
        ]
        scores = [dot_nt(part(here, which, 1), queries[which]) for which in range(pairs)]
        grad_probs = [dot_nt(part(here, which, 2), grads[which]) for which in range(pairs)]
        keys = [part(here, which, 1) for which in range(pairs)]
        return (
            queries, grads, keys, jnp.concatenate(scores, axis=1),
            jnp.concatenate(grad_probs, axis=1),
        )

    groups = list(group_rows(rows))
    products = products_of(groups[0])
    for index, here in enumerate(groups):
        queries, grads, keys, scores, grad_probs = products
        if index + 1 < len(groups):
            products = products_of(groups[index + 1])
        probs = group_softmax(scores, bias)
        inner = jnp.sum(probs * grad_probs, axis=0, keepdims=True)
        grad_scores = to_low(probs * (grad_probs - inner))
        probs = to_low(probs)
        results = []
        for which in range(pairs):
            lanes = slice(which * pair, (which + 1) * pair)
            own = grad_scores[:, lanes]
            both = dot_tn(own, keys[which]) * scale
            results.append((
                jnp.where(lane < pair // 2, both[:GROUP], both[GROUP:]),
                dot(own, queries[which]),
                dot(probs[:, lanes], grads[which]),
            ))
        for which in range(pairs):
            for kind in range(3):
                start = kind * width + which * pair
                grad_qkv_ref[here, start : start + pair] = to_low(results[which][kind])


def attention_backward(qkv, grad, after=()):
    total, width = grad.shape
    rows = total // ROW_STEPS

    def by_rows(columns):
        return pl.BlockSpec((rows, columns), lambda step: (step, 0))

    return call(
        attention_backward_kernel,
        (ROW_STEPS,),
        [by_rows(3 * width), by_rows(width)],
        [by_rows(3 * width)],
        [shape((total, 3 * width), jnp.bfloat16)],
        [],
        (qkv, grad),
        total * width * width * 8,
        after,
    )[0]


def first_weight_kernel(split, pos_ref, norm_ref, mixed_ref, low_ref, grad_ref, *refs):
    count = len(split.specs())
    grad_refs, scr = refs[:count], refs[count:]
    step = pl.program_id(0)

    @pl.when(step < 3)
    def _():
        split.store(dot(norm_ref[...], grad_ref[...]), grad_refs, scr, pos_ref)

    @pl.when(step == 3)
    def _():
        split.store(dot_tn(mixed_ref[...], low_ref[...]), grad_refs, scr, pos_ref)


def first_weight(norm, mixed, low, grad, place, pos, after=()):
    width, total = norm.shape
    split = Split(place, width, width)
    return call(
        functools.partial(first_weight_kernel, split),
        (4,),
        [
            whole(norm), whole(mixed), whole(low),
            pl.BlockSpec((total, width), lambda step, pos: (0, jnp.minimum(step, 2))),
        ],
        split.specs(),
        split.outs(4),
        split.scratch(),
        (norm, mixed, low, grad),
        8 * total * width * width * 1.5,
        after,
        pos,
        large=(0, 1),
    )


def states_backward_kernel(grad_ref, grad_x_ref, x_ref, gain_ref, w_ref, out_ref, grad_gain_ref):
    parts = blocks_of(x_ref.shape[0], 208)
    grads = [dot_nt(grad_ref[here, :], w_ref[...]) for here in parts]
    results = []
    grad_gain = 0.0
    for here, grad_a in zip(parts, grads):
        hat, inverse = normalize(wide(x_ref[here, :]))
        grad_gain = grad_gain + jnp.sum(grad_a * hat, axis=0, keepdims=True)
        results.append(
            grad_x_ref[here, :] + norm_back(grad_a * gain_ref[0:1, :], hat, inverse)
        )
    for here, result in zip(parts, results):
        out_ref[here, :] = result

    @pl.when(pl.program_id(0) == 0)
    def _():
        grad_gain_ref[...] = grad_gain

    @pl.when(pl.program_id(0) > 0)
    def _():
        grad_gain_ref[...] += grad_gain


def states_backward(grad, grad_x, states, gains, weights, after=()):
    total, width = states.shape
    rows = total // ROW_STEPS

    def by_rows(columns):
        return pl.BlockSpec((rows, columns), lambda step: (step, 0))

    return call(
        states_backward_kernel,
        (ROW_STEPS,),
        [
            by_rows(3 * width),
            by_rows(width),
            by_rows(width),
            whole(gains),
            pl.BlockSpec((width, 3 * width), lambda step: (0, 0)),
        ],
        [by_rows(width), pl.BlockSpec((1, width), lambda step: (0, 0))],
        [shape((total, width)), shape((1, width))],
        [],
        (grad, grad_x, states, gains, weights),
        6 * total * width * width * 1.5,
        after,
    )


def stats_kernel(place, edges, pos_ref, stats_ref, gain_ref, *refs):
    count = 3 if place is None else 3 * place.groups
    grad_refs, refs = refs[:count], refs[count:]
    full_ref, new_rows_ref, sums_ref = refs
    blocks = edges[-1]
    width = full_ref.shape[1] // blocks
    piece = full_ref.shape[1] // 3
    for which in range(3):
        if place is None:
            full_ref[:, which * piece : (which + 1) * piece] = wide(grad_refs[which][0])
            continue
        for mask in range(place.groups):
            part = piece // place.groups
            column = pl.multiple_of(which * piece + (pos_ref[2] ^ mask) * part, part)
            full_ref[:, pl.ds(column, part)] = wide(
                grad_refs[which * place.groups + mask][0, : full_ref.shape[0]]
            )
    sums_ref[...] = jnp.zeros_like(sums_ref)
    lane = iota((1, width), 1)
    tail = jnp.zeros((1, width), jnp.float32)
    for which in range(4):
        lower, upper = edges[which], edges[which + 1]
        total = 0.0
        for block in range(lower, upper):
            part = full_ref[:, block * width : (block + 1) * width]
            squares = part * part + STAT_EPSILON
            sums_ref[block : block + 1, :] = jnp.sum(squares, axis=0, keepdims=True)
            total = total + jnp.sum(squares, axis=1, keepdims=True)
        mean = total * (1.0 / ((upper - lower) * width))
        rows = 0.5 * stats_ref[:, which : which + 1] + 0.5 * mean
        new_rows_ref[:, which : which + 1] = rows
        tail = jnp.where(lane == which, jnp.sum(rows, axis=0, keepdims=True), tail)
        inverse = 1.0 / rows
        for block in range(lower, upper):
            part = full_ref[:, block * width : (block + 1) * width]
            sums_ref[blocks + block : blocks + block + 1, :] = jnp.sum(
                part * part * inverse, axis=0, keepdims=True
            )
    sums_ref[2 * blocks : 2 * blocks + 1, :] = tail
    if place is None:
        gain = gain_ref[...]
    else:
        terms = [wide(ref[0, full_ref.shape[0] :]) for ref in grad_refs[: place.groups]]
        terms = (terms[0] + terms[1]) + (terms[2] + terms[3])
        gain = terms[0:2] + terms[2:4] + terms[4:6]
    sums_ref[2 * blocks + 1 : 2 * blocks + 3, :] = gain


def gradient_stats(grads, stats, gain_grad, bounds, place, pos, after=()):
    rows = stats.shape[1]
    width = bounds[2] - bounds[1]
    edges = tuple(bound // width for bound in bounds)
    outs = [
        shape((rows, bounds[-1])), shape((rows, 4)),
        shape((-(-(2 * edges[-1] + 3) // 8) * 8, width)),
    ]
    args = (stats.T, gain_grad, *(array for array, _ in grads))
    return call(
        functools.partial(stats_kernel, place, edges),
        (1,),
        [whole(arg) for arg in args[:2]] + [some(array, at, 1) for array, at in grads],
        [whole(out) for out in outs],
        outs,
        [],
        args,
        10 * rows * bounds[-1],
        after,
        pos,
    )


def update_kernel(
    edges, sums_ref, old_cols_ref, rows_ref, gain_stats_ref,
    grad_ref, old_ref,
    new_ref, low_ref, new_cols_ref, ratio_ref, gain_ref, new_gain_stats_ref, gain_update_ref,
    factor_scr, cols_scr,
):
    step = pl.program_id(0)
    blocks = edges[-1]
    width = sums_ref.shape[1]
    per_step = new_ref.shape[1] // width

    @pl.when(step == 0)
    def _():
        new_cols = 0.5 * old_cols_ref[...] + 0.5 * (sums_ref[:blocks, :] * (1.0 / width))
        new_cols_ref[...] = new_cols
        cols_scr[...] = lax.rsqrt(new_cols)
        scaled = sums_ref[blocks : 2 * blocks, :] / new_cols
        lane = iota((1, ratio_ref.shape[1]), 1)
        ratios = jnp.zeros(ratio_ref.shape, jnp.float32)
        for which in range(4):
            lower, upper = edges[which], edges[which + 1]
            mean = sums_ref[2 * blocks : 2 * blocks + 1, which : which + 1] * (1.0 / width)
            total = jnp.sum(jnp.sum(scaled[lower:upper], axis=0, keepdims=True), axis=1, keepdims=True)
            total = total * mean * (1.0 / (width * width * (upper - lower)))
            ratio = jnp.maximum(1.0, jnp.sqrt(total) / CLIP_LEVEL)
            ratios = jnp.where(lane == which, ratio, ratios)
            factor = (WEIGHT_RATE / ratio) * lax.rsqrt(rows_ref[:, which : which + 1] / mean)
            for block in range(lower, upper):
                factor_scr[block] = factor
        gain = sums_ref[2 * blocks + 1 : 2 * blocks + 3, :]
        gain_ref[...] = gain
        new_stats = 0.5 * gain_stats_ref[...] + 0.5 * (gain * gain + STAT_EPSILON)
        new_gain_stats_ref[...] = new_stats
        update = gain * lax.rsqrt(new_stats)
        total = jnp.sum(update * update, axis=1, keepdims=True) * (1.0 / width)
        gain_ratios = jnp.maximum(1.0, jnp.sqrt(total) / CLIP_LEVEL)
        gain_update_ref[...] = GAIN_RATE * update / gain_ratios
        for which in range(2):
            ratios = jnp.where(lane == 4 + which, gain_ratios[which : which + 1, :], ratios)
        ratio_ref[...] = ratios

    for block in range(per_step):
        lanes = slice(block * width, (block + 1) * width)
        index = step * per_step + block
        scale = cols_scr[pl.ds(index, 1), :]
        new = old_ref[:, lanes] - grad_ref[:, lanes] * scale * factor_scr[index]
        new_ref[:, lanes] = new
        low_ref[:, lanes] = to_low(new)


def update_weights(grad, old, sums, old_cols, new_rows, gain_stats, bounds, after=()):
    rows, total = grad.shape
    width = bounds[2] - bounds[1]
    edges = tuple(bound // width for bound in bounds)
    steps = 3
    args = (sums, old_cols.reshape(-1, width), new_rows, gain_stats)
    outs = [
        shape((rows, total)), shape((rows, total), jnp.bfloat16),
        shape((edges[-1], width)), shape((1, 6)),
    ] + [shape(gain_stats.shape)] * 3
    by_columns = pl.BlockSpec((rows, total // steps), lambda step: (0, step))
    return call(
        functools.partial(update_kernel, edges),
        (steps,),
        [whole(arg) for arg in args] + [by_columns, by_columns],
        [by_columns, by_columns] + [whole(out) for out in outs[2:]],
        outs,
        [
            pltpu.VMEM((edges[-1], rows, 1), jnp.float32),
            pltpu.VMEM((edges[-1], width), jnp.float32),
        ],
        (*args, grad, old),
        10 * rows * total,
        after,
    )


def cut_kernel(counts, pos_ref, *refs):
    at = 0
    for count, out in zip(counts, refs[sum(counts) :]):
        for index in range(count):
            out[index] = to_low(refs[at + index][...])
        at += count


def cut(weights, groups, width, pos):
    rows = weights.shape[0]
    counts = (1, 2, 2)
    places = [lambda group: group]
    for piece in (1, 2):
        for side in (0, 1):
            places.append(
                lambda group, piece=piece, side=side: piece * groups
                + 2 * side
                + ((group >> side) & 1)
            )
    outs = [shape((count, rows, width), jnp.bfloat16) for count in counts]
    return call(
        functools.partial(cut_kernel, counts),
        (1,),
        [
            pl.BlockSpec((rows, width), lambda step, pos, at=at: (0, at(pos[2])))
            for at in places
        ],
        [whole(a) for a in outs],
        outs,
        [],
        (weights,) * len(places),
        len(places) * rows * width,
        (),
        pos,
        vmem=VMEM_MOST,
    )


def line_gather(own, chips):
    return [own] + [swap(own, "shard", 2 * mask) for mask in range(1, chips)]


def arrange_kernel(plan, count, *refs):
    for parts, out in zip(plan, refs[count:]):
        at = 0
        for which, start, stop in parts:
            out[at : at + stop - start] = refs[which][start:stop]
            at += stop - start


def arrange(plan, args, after=()):
    outs = [
        shape((sum(stop - start for _, start, stop in parts),) + args[parts[0][0]].shape[1:],
              args[parts[0][0]].dtype)
        for parts in plan
    ]
    return call(
        functools.partial(arrange_kernel, plan, len(args)),
        (1,),
        [whole(a) for a in args],
        [whole(a) for a in outs],
        outs,
        [],
        args,
        sum(a.size for a in outs),
        after,
        least=0,
    )


class Gather:
    def __init__(self, place, lines, quarters, columns):
        halves = len(quarters) == 2
        self.place = Place(place.chips, place.rows, place.groups, halves=halves)
        self.lines, self.columns = lines, columns
        self.blocks = list(quarters)
        if halves:
            self.blocks += [swap(quarter, "group", k + 1) for k, quarter in enumerate(quarters)]
        else:
            self.blocks += [swap(quarters[0], "group", mask) for mask in range(1, place.groups)]

    def weights(self, joined):
        masks = tuple(range(self.place.groups))
        keys = [(self.lines, (mask,), True) for mask in masks] + [(self.lines, masks, False)]
        return Weights(
            self.place, self.blocks + [in_hbm(swap(joined, "shard", 1))], keys, self.columns
        )


class RelayGather:
    def __init__(self, place, lines, quarter, columns):
        self.place, self.lines, self.columns = place, lines, columns
        self.blocks = [quarter] + [swap(quarter, "group", mask) for mask in (1, 2)]

    def plan(self):
        count = self.place.chips
        return [
            [(1, 0, count // 2)],
            [(2, count // 2, count)],
            [(0, 0, count), (1, 0, count), (2, 0, count)],
        ]

    def send_far(self, far_x, far_y, joined):
        self.far = [swap(far_x, "group", 2), swap(far_y, "group", 1)]
        self.joined = in_hbm(swap(joined, "shard", 1))

    def weights(self, corner):
        lines, half = self.lines, self.place.chips // 2
        arrays = self.blocks + self.far + [self.joined, swap(corner, "shard", 1)]
        keys = [(lines, (mask,), True) for mask in (0, 1, 2)]
        keys += [(lines[:half], (3,), True), (lines[half:], (3,), True)]
        keys += [(lines, (0, 1, 2), False), (lines, (3,), False)]
        return Weights(self.place, arrays, keys, self.columns)


def swap_blocks(blocks):
    return [swap(block, "shard", 2 * mask) for mask, block in enumerate(blocks, 1)]


def add_blocks(out, at, parts):
    total = 0.0
    for ref, place in parts:
        total = total + wide(ref[place + (Ellipsis,)])
    out[at + (Ellipsis,)] = total.astype(out.dtype)


def plane_blocks_kernel(*refs):
    count = len(refs) // 3
    for mine_ref, theirs_ref, out in zip(refs[:count], refs[count:], refs[2 * count :]):
        out[...] = to_low(wide(mine_ref[0]) + wide(theirs_ref[0]))


def far_kernel(mine_ref, theirs_ref, first_ref, second_ref):
    half = first_ref.shape[0]
    for line in range(2 * half):
        out = first_ref if line < half else second_ref
        add_blocks(out, (line % half,), [(mine_ref, (0, line)), (theirs_ref, (0, line))])


def near_kernel(mine_1, mine_2, theirs_1, theirs_2, far_x_ref, far_y_ref, first_ref, second_ref):
    half = far_x_ref.shape[0]
    for line in range(2 * half):
        first = [(mine_1, (0, line)), (theirs_1, (0, line))]
        second = [(mine_2, (0, line)), (theirs_2, (0, line))]
        if line < half:
            second.append((far_x_ref, (line,)))
        else:
            first.append((far_y_ref, (line - half,)))
        add_blocks(first_ref, (line,), first)
        add_blocks(second_ref, (line,), second)


def line_kernel(count, mine_ref, theirs_ref, *refs):
    received, out_refs = refs[:count], refs[count:]
    for line, out in enumerate(out_refs):
        parts = [(mine_ref, (0, line)), (theirs_ref, (0, line))]
        add_blocks(out, (), parts + [(ref, (line,)) for ref in received])


def final_kernel(counts, *refs):
    out_ref = refs[-1]
    at = 0
    for index, count in enumerate(counts):
        add_blocks(out_ref, (index,), [(ref, ()) for ref in refs[at : at + count]])
        at += count


GAIN_ROWS = 16


def gain_terms(gain):
    dims = (GAIN_ROWS, gain.shape[1])
    row = iota(dims, 0)
    rest = jnp.where((row & 1) == 0, gain[0:1, :], gain[1:2, :])
    terms = jnp.zeros(dims, jnp.float32)
    for which in range(3):
        term = wide(to_low(rest))
        terms = jnp.where(lax.shift_right_logical(row, 1) == which, term, terms)
        rest = rest - term
    return to_low(terms)


def last_kernel(gain_ref, *refs):
    out_ref = refs[-1]
    rows = refs[0].shape[0]
    total = refs[0][...]
    for ref in refs[1:-1]:
        total = total + wide(ref[...])
    out_ref[0, :rows] = to_low(total)
    out_ref[0, rows:] = gain_terms(gain_ref[...])


def finish_last(gain, piece, after=()):
    rows, columns = piece[0].shape
    out = shape((1, rows + GAIN_ROWS, columns), jnp.bfloat16)
    args = (gain, *piece)
    return call(
        last_kernel,
        (1,),
        [whole(a) for a in args],
        [whole(out)],
        [out],
        [],
        args,
        out.size,
        after,
        least=0,
    )[0]


def finish(pieces, after=(), least=0):
    out = shape((len(pieces),) + pieces[0][0].shape, jnp.bfloat16)
    args = tuple(a for piece in pieces for a in piece)
    return call(
        functools.partial(final_kernel, tuple(len(piece) for piece in pieces)),
        (1,),
        [whole(a) for a in args],
        [whole(out)],
        [out],
        [],
        args,
        out.size,
        after,
        least=least,
    )[0]


def pair_line_kernel(count, mine_ref, theirs_ref, *refs):
    received, (own_ref, kept_ref, sent_ref) = refs[:count], refs[count:]
    for line in range(4):
        out, at = ((own_ref, ()), (sent_ref, (0,)), (kept_ref, ()), (sent_ref, (1,)))[line]
        parts = [(mine_ref, (0, line)), (theirs_ref, (0, line))]
        add_blocks(out, at, parts + [(ref, (line,)) for ref in received])


def far_line_kernel(own_ref, kept_ref, received_ref, total_ref, sent_ref):
    add_blocks(total_ref, (), [(own_ref, ()), (received_ref, (0,))])
    add_blocks(sent_ref, (), [(kept_ref, ()), (received_ref, (1,))])


class Reduction:
    def __init__(self, place, mine, theirs):
        self.place, self.mine = place, mine
        self.theirs = in_hbm(swap(theirs, "shard", 1))
        self.block = mine.shape[1:]

    def send_plane(self, after=()):
        outs = [shape(self.block, jnp.bfloat16)] * (self.place.groups - 1)
        args = (self.mine,) * len(outs) + (self.theirs,) * len(outs)
        self.sent = call(
            plane_blocks_kernel, (1,),
            [some(self.mine, index % len(outs) + 1, 1) for index in range(len(args))],
            [whole(a) for a in outs], outs, [], args, self.mine.size, after,
        )
        self.plane = [swap(block, "group", mask) for mask, block in enumerate(self.sent, 1)]

    def send(self, kernel, specs, dims, args, after):
        out = shape(dims, jnp.bfloat16)
        return call(
            kernel, (1,), specs, [whole(out)] * 2, [out, out], [], args, self.mine.size, after,

        )

    def send_far(self, after=()):
        args = (self.mine, self.theirs)
        half = (self.block[0] // 2,) + self.block[1:]
        self.sent = self.send(far_kernel, [some(a, 3, 1) for a in args], half, args, after)
        self.far = [swap(self.sent[0], "group", 1), swap(self.sent[1], "group", 2)]

    def send_near(self, after=()):
        args = (self.mine, self.mine, self.theirs, self.theirs, *self.far)
        specs = [some(self.mine, which % 2 + 1, 1) for which in range(4)]
        specs += [whole(a) for a in self.far]
        self.sent = self.send(near_kernel, specs, self.block, args, after)
        self.plane = [swap(self.sent[0], "group", 1), swap(self.sent[1], "group", 2)]

    def send_lines(self, after=()):
        args = (self.mine, self.theirs, *self.plane)
        specs = [some(a, 0, 1) for a in args[:2]] + [whole(a) for a in args[2:]]
        outs = [shape(self.block[1:])]
        outs += [shape(self.block[1:], jnp.bfloat16)] * (self.block[0] - 1)
        self.own, *self.sent_lines = call(
            functools.partial(line_kernel, len(self.plane)), (1,), specs,
            [whole(a) for a in outs], outs, [], args, self.mine.size, after,
        )
        self.lines = swap_blocks(self.sent_lines)

    def send_pair(self, after=()):
        args = (self.mine, self.theirs, *self.plane)
        specs = [some(a, 0, 1) for a in args[:2]] + [whole(a) for a in args[2:]]
        one = self.block[1:]
        outs = [shape(one), shape(one), shape((2,) + one, jnp.bfloat16)]
        self.own, self.kept, self.sent = call(
            functools.partial(pair_line_kernel, len(self.plane)), (1,), specs,
            [whole(a) for a in outs], outs, [], args, self.mine.size, after,
        )
        self.received = swap(self.sent, "shard", 2)

    def send_line(self, after=()):
        args = (self.own, self.kept, self.received)
        outs = [shape(self.own.shape), shape(self.own.shape, jnp.bfloat16)]
        self.own, self.sent = call(
            far_line_kernel, (1,), [whole(a) for a in args], [whole(a) for a in outs], outs, [],
            args, self.own.size, after,
        )
        self.lines = [swap(self.sent, "shard", 4)]


def lines_kernel(*refs):
    count = len(refs) // 3
    for mine_ref, theirs_ref, out in zip(refs[:count], refs[count:], refs[2 * count :]):
        out[0] = to_low(wide(mine_ref[0, 0]) + wide(theirs_ref[0, 0]))


def first_plane_kernel(mine_ref, theirs_ref, *refs):
    received, (own_ref, kept_ref, sent_ref) = refs[:-3], refs[-3:]
    for index in range(4):
        out, at = ((own_ref, ()), (sent_ref, (0,)), (kept_ref, ()), (sent_ref, (1,)))[index]
        parts = [(mine_ref, (0, index)), (theirs_ref, (0, index))]
        add_blocks(out, at, parts + [(ref, (index,)) for ref in received])


class LineReduction:
    def __init__(self, place, mine, theirs):
        self.place, self.mine = place, mine
        self.theirs = in_hbm(swap(theirs, "shard", 1))

    def line_view(self, line):
        block = (1, 1) + self.mine.shape[2:]
        return pl.BlockSpec(block, lambda step: (line, step, 0, 0))

    def send_lines(self, after=()):
        chips, groups, rows, columns = self.mine.shape
        others = range(1, chips)
        out = pl.BlockSpec((1, rows, columns), lambda step: (step, 0, 0))
        self.sent = call(
            lines_kernel, (groups,), [self.line_view(line) for line in others] * 2,
            [out] * len(others), [shape((groups, rows, columns), jnp.bfloat16)] * len(others), [],
            (self.mine,) * len(others) + (self.theirs,) * len(others), self.mine.size, after,
        )
        self.lines = swap_blocks(self.sent)

    def send_first(self, after=()):
        one = self.mine.shape[2:]
        outs = [shape(one), shape(one), shape((2,) + one, jnp.bfloat16)]
        args = (self.mine, self.theirs, *self.lines)
        specs = [some(a, 0, 1) for a in args[:2]] + [whole(a) for a in args[2:]]
        self.own, self.kept, self.sent = call(
            first_plane_kernel, (1,), specs, [whole(a) for a in outs], outs, [],
            args, self.mine.size, after,
        )
        self.received = swap(self.sent, "group", 1)

    def send_second(self, after=()):
        args = (self.own, self.kept, self.received)
        outs = [shape(self.own.shape), shape(self.own.shape, jnp.bfloat16)]
        self.own, self.sent = call(
            far_line_kernel, (1,), [whole(a) for a in args], [whole(a) for a in outs], outs, [],
            args, self.own.size, after,
        )
        self.plane = [swap(self.sent, "group", 2)]


def swap(value, axis, mask):
    size = lax.axis_size(axis)
    return lax.ppermute(value, axis, [(place, place ^ mask) for place in range(size)])


def in_hbm(array):
    return pltpu.with_memory_space_constraint(array, pltpu.MemorySpace.HBM)


def place_at(parts, positions, axis):
    out = jnp.zeros((len(parts),) + parts[0].shape, parts[0].dtype)
    for part, position in zip(parts, positions):
        out = lax.dynamic_update_slice_in_dim(out, part[None], position, 0)
    return out


def gather_piece(piece):
    groups, shards_count = lax.axis_size("group"), lax.axis_size("shard")
    group, shard = lax.axis_index("group"), lax.axis_index("shard")
    far, core = shard // 2, shard % 2
    chips = shards_count // 2
    rows, width = piece.shape
    part_width = width // groups
    own = to_low(lax.dynamic_slice_in_dim(piece, group * part_width, part_width, 1))
    line = [own] + [swap(own, "shard", 2 * mask) for mask in range(1, chips)]
    quarter = place_at(line, [far ^ mask for mask in range(chips)], 0)
    plane = [quarter] + [swap(quarter, "group", mask) for mask in range(1, groups)]
    half = jnp.zeros((chips, rows, width), quarter.dtype)
    for mask in range(groups):
        half = lax.dynamic_update_slice_in_dim(half, plane[mask], (group ^ mask) * part_width, 2)
    other = swap(half, "shard", 1)
    low = jnp.where(core == 0, half, other)
    high = jnp.where(core == 0, other, half)
    return jnp.stack([low, high], axis=1).reshape(shards_count * rows, width)


def reduce_piece(grad):
    groups, shards_count = lax.axis_size("group"), lax.axis_size("shard")
    group, shard = lax.axis_index("group"), lax.axis_index("shard")
    far, core = shard // 2, shard % 2
    chips = shards_count // 2
    width = grad.shape[1]
    rows = grad.shape[0] // shards_count
    part_width = width // groups
    view = grad.reshape(chips, 2, rows, width)
    theirs = to_low(lax.dynamic_index_in_dim(view, 1 - core, 1, keepdims=False))
    mine = lax.dynamic_index_in_dim(view, core, 1, keepdims=False)
    chip_sum = mine.astype(jnp.float32) + swap(theirs, "shard", 1).astype(jnp.float32)

    def columns(which):
        return lax.dynamic_slice_in_dim(chip_sum, which * part_width, part_width, 2)

    plane = [swap(to_low(columns(group ^ mask)), "group", mask) for mask in range(1, groups)]
    plane_sum = columns(group)
    for value in plane:
        plane_sum = plane_sum + value.astype(jnp.float32)

    def line_block(which):
        return lax.dynamic_index_in_dim(plane_sum, which, 0, keepdims=False)

    line = [swap(to_low(line_block(far ^ mask)), "shard", 2 * mask) for mask in range(1, chips)]
    total = line_block(far)
    for value in line:
        total = total + value.astype(jnp.float32)
    total = to_low(total)
    out = jnp.zeros((rows, width), total.dtype)
    for mask in range(groups):
        part = swap(total, "group", mask) if mask else total
        out = lax.dynamic_update_slice_in_dim(out, part, (group ^ mask) * part_width, 1)
    return out


def masks_of(size):
    mask = 1
    while mask < size:
        yield mask
        mask *= 2


def sum_over(value, axis):
    for mask in masks_of(lax.axis_size(axis)):
        value = value + swap(value, axis, mask)
    return value


def spread_columns(array):
    count = lax.axis_size("shard")
    columns = array.shape[1]
    out = jnp.zeros((array.shape[0], columns * count), array.dtype)
    return lax.dynamic_update_slice_in_dim(out, array, lax.axis_index("shard") * columns, 1)


def own_columns(array):
    columns = array.shape[1] // lax.axis_size("shard")
    return lax.dynamic_slice_in_dim(array, lax.axis_index("shard") * columns, columns, 1)


def gather_embeds(low):
    value = low
    shard, group = lax.axis_index("shard"), lax.axis_index("group")
    steps = [("shard", mask, shard) for mask in masks_of(lax.axis_size("shard")) if mask > 1]
    steps += [("group", mask, group) for mask in masks_of(lax.axis_size("group"))]
    steps += [("shard", 1, shard)]
    for axis, mask, index in steps:
        other = swap(value, axis, mask)
        upper = (index & mask) != 0
        value = jnp.concatenate(
            [jnp.where(upper, other, value), jnp.where(upper, value, other)], axis=0
        )
    return value


def shards(
    image_states,
    text_states,
    image_weights,
    image_gains,
    text_weights,
    text_gains,
    logit_scale,
    pair_ids,
    row_stats,
    col_stats,
    gain_stats,
):
    rows, model_width = text_weights.shape[0], text_states.shape[1]
    hidden = (text_weights.shape[1] - 4 * model_width) // 2
    bounds = (
        0,
        3 * model_width,
        4 * model_width,
        4 * model_width + hidden,
        4 * model_width + 2 * hidden,
    )
    groups, chips = lax.axis_size("group"), lax.axis_size("shard") // 2
    group, shard = lax.axis_index("group"), lax.axis_index("shard")
    pos = jnp.stack([shard // 2, shard % 2, group]).astype(jnp.int32)
    own_pairs = pair_ids.shape[0]
    scale = logit_scale.reshape(1, 1)
    place = None
    if rows % 16 == 0 and groups == 4 and chips == 4 and hidden == 4 * model_width:
        place = Place(chips, rows, groups)

    rounded_gains = lax.reduce_precision(text_gains, exponent_bits=8, mantissa_bits=7)
    gain_rows = jnp.concatenate([rounded_gains, gain_stats])
    gain_rows = spread_columns(gain_rows)
    lead = ()
    if place is not None:
        width = hidden // groups
        own_first, own_up, own_down = cut(text_weights, groups, width, pos)
        line = line_gather(own_first, chips)
        high_up = swap(own_up, "shard", 4)
    class_rows = image_attention(image_states, image_weights, image_gains)
    if place is not None:
        quarter, own_down, gain_rows = arrange(
            [[(k, 0, 1) for k in range(4)], [(4, 0, 2)], [(5, 0, 1)]],
            (*line, own_down, gain_rows[None]),
            after=(class_rows,),
        )
        first_piece = RelayGather(place, (0, 1, 2, 3), quarter, hidden)
        gain_rows = gain_rows + swap(gain_rows, "shard", 1)
        (pair,) = arrange([[(0, 0, 2), (1, 0, 2)]], (own_up, high_up), (quarter,))
        low_up = swap(pair, "shard", 2)
        high_down = swap(own_down, "shard", 4)
        lead = (quarter, pair)
    image_embed, image_low = image_mlp(
        class_rows, image_weights, image_gains, own_pairs, after=lead
    )
    padded = image_low.shape[0]
    total_pairs = padded * groups * chips * 2
    image_bias = np.where(np.arange(total_pairs) % padded < own_pairs, 0.0, MASKED)
    image_bias = jnp.asarray(image_bias[None], jnp.float32)

    if place is None:
        for mask in masks_of(2 * chips):
            gain_rows = gain_rows + swap(gain_rows, "shard", mask)
        gains, all_gain_stats = gain_rows[:2], gain_rows[2:]
        w_first, w_up, w_down = (
            Weights(None, [gather_piece(text_weights[:, lower:upper])[None]], None, upper - lower)
            for lower, upper in ((0, bounds[2]), bounds[2:4], bounds[3:5])
        )
        images = Weights(None, [gather_embeds(image_low)[None]], None, model_width)
        own_block = (shard % 2) * (groups * chips) + group * chips + shard // 2
        qkv, full_first = project(text_states, w_first, gains, pos)
        mixed, first = attention_forward(text_states, qkv, full_first)
        hidden_sum, slope, pooled, full_up = up_forward(first, w_up, gains, pos)
    else:
        own_block = shard * groups + group
        order = (0, 2, 1, 3)
        masks = tuple(range(groups))

        def quarter_plan(which, at):
            plan = [(at, which, which + 1), (at + 1, which, which + 1)]
            return plan + [(at + 2, which, which + 1), (at + 2, which + 2, which + 3)]

        join_plan = [(k, 0, chips) for k in masks]
        half = chips // 2
        far_x, far_y, joined, *quarters, image_own, gain_rows = arrange(
            first_piece.plan() + [quarter_plan(0, 3), quarter_plan(1, 3), [(6, 0, 1)], [(7, 0, 1)]],
            (*first_piece.blocks, own_up, high_up, low_up, image_low[None], gain_rows),
        )
        first_piece.send_far(far_x, far_y, joined)
        image_high = swap(image_own, "shard", 4)
        gain_rows = gain_rows + swap(gain_rows, "shard", 2)
        corner, *quarters, gain_rows, image_pair = arrange(
            [[(0, 0, half), (1, 0, half)], [(2, 0, chips)], [(3, 0, chips)]]
            + [[(4, 0, 1)], [(5, 0, 1), (6, 0, 1)]],
            (*first_piece.far, *quarters, gain_rows, image_own, image_high),
        )
        w_first = first_piece.weights(corner)
        up_piece = Gather(place, order, quarters, hidden)
        image_lower = swap(image_pair, "shard", 2)
        gain_rows = (gain_rows + swap(gain_rows, "shard", 4))[0]
        gains, all_gain_stats = gain_rows[:2], gain_rows[2:]
        qkv, full_first = project(text_states, w_first, gains, pos)
        image_quarter, pair = arrange(
            [[(0, 0, 2), (1, 0, 2)], [(2, 0, 2), (3, 0, 2)]],
            (image_pair, image_lower, own_down, high_down),
            after=(qkv,),
        )
        low_down = swap(pair, "shard", 2)
        image_blocks = [image_quarter] + [swap(image_quarter, "group", mask) for mask in (1, 2)]
        mixed, first = attention_forward(text_states, qkv, full_first, after=(image_quarter,))
        joined, far_x, far_y, *quarters = arrange(
            [join_plan, [(groups, 0, half)], [(groups + 1, half, chips)]]
            + [quarter_plan(0, groups + 2), quarter_plan(1, groups + 2)],
            (*up_piece.blocks, *image_blocks[1:], own_down, high_down, low_down),
            after=(first,),
        )
        image_blocks += [swap(far_x, "group", 2), swap(far_y, "group", 1)]
        w_up = up_piece.weights(joined)
        down_piece = Gather(place, order, quarters, hidden)
        hidden_sum, slope, pooled, full_up = up_forward(
            first, w_up, gains, pos, after=tuple(quarters)
        )
        joined, image_joined = arrange(
            [join_plan]
            + [[(groups + k, 0, chips) for k in (0, 1, 2)] + [(7, 0, half), (8, 0, half)]],
            (*down_piece.blocks, *image_blocks),
            after=(hidden_sum,),
        )
        w_down = down_piece.weights(joined)
        images = Weights(
            Place(chips, padded, groups, stacked=True),
            image_blocks + [in_hbm(swap(image_joined, "shard", 1))],
            [(order, (mask,), True) for mask in (0, 1, 2)]
            + [(order[:half], (3,), True), (order[half:], (3,), True), (order, masks, False)],
            model_width,
        )
    text_embed, pooled_inv, scores, row_total, col_total, full_down, all_image = scores_forward(
        hidden_sum, pooled, w_down, images, image_bias, scale, pos
    )
    norm_up = turned_norm(first, gains, 1, after=(col_total,))
    if place is None:
        rounds = [(axis, (mask,)) for axis in ("shard", "group") for mask in masks_of(lax.axis_size(axis))]
    else:
        rounds = [("shard", (1,)), ("shard", (2, 4, 6)), ("group", (1, 2, 3))]
    for axis, near in rounds:
        received = [swap(col_total, axis, mask) for mask in near]
        for value in received:
            col_total = jnp.logaddexp(col_total, value)
    target = (own_block * padded + pair_ids)[:, None]
    grad_hidden, grad_out, grads_down = scores_backward(
        scores, row_total, col_total, target, scale, all_image, text_embed, pooled_inv,
        hidden_sum, full_down, place, pos, after=(norm_up,),
    )
    norm_first = turned_norm(text_states, gains, 0, after=(grad_out,))
    after = [()] * 4
    if place is not None:
        down = Reduction(place, *grads_down)
        down.send_plane(after=(norm_first,))
        after[0] = tuple(down.sent)
    grad_b, grads_up = up_backward(
        grad_hidden, slope, norm_up, full_up, place, pos, after=after[0]
    )
    grad_first, grad_low, grad_mixed, grad_gain_up = first_backward(
        grad_b, grad_out, first, gains, full_first
    )
    if place is not None:
        up = Reduction(place, *grads_up)
        up.send_far(after=(grad_low,))
        after[1] = tuple(up.sent)
    grad_qkv = attention_backward(qkv, grad_mixed, after=after[1])
    if place is not None:
        down.send_pair(after=(grad_qkv,))
        up.send_near(after=(down.sent,))
        after[2] = tuple(up.sent)
    grads_first = first_weight(norm_first, mixed, grad_low, grad_qkv, place, pos, after=after[2])
    if place is not None:
        last = Reduction(place, *grads_first)
        after[3] = (grads_first[0],)
    grad_states, grad_gain_first = states_backward(
        grad_qkv, grad_first, text_states, gains, full_first, after=after[3]
    )
    gain_total = jnp.concatenate([grad_gain_first, grad_gain_up], axis=0)
    if place is not None:
        last.send_plane(after=(grad_states,))
        up.send_pair(after=tuple(last.sent))
        down.send_line(after=(up.sent,))
        up.send_line(after=(down.sent,))
        others = finish([[up.own] + up.lines, [down.own] + down.lines])
        near = [swap(others, "group", mask) for mask in (1, 2)]
        last.send_lines(after=(others,))
        result = finish_last(gain_total, [last.own] + last.lines)
        pieces = [(result, 0)] + [
            (swap(result, "group", mask), 0) for mask in range(1, groups)
        ]
        blocks = [others, *near, swap(near[0], "group", 2)]
        pieces += [(block, which) for which in (0, 1) for block in blocks]
    else:
        gain_total = sum_over(gain_total, "group")
        pieces = [
            (reduce_piece(grads[0])[None], 0) for grads in (grads_first, grads_up, grads_down)
        ]
    weight_grad, new_rows, sums = gradient_stats(
        pieces, row_stats, gain_total, bounds, place, pos
    )
    sums = sum_over(sums, "shard")
    new_weights, new_low, new_cols, ratios, gain_grad, new_gain_stats, gain_update = (
        update_weights(
            in_hbm(weight_grad), in_hbm(text_weights), sums, col_stats, new_rows, all_gain_stats,
            bounds,
        )
    )
    new_gains = text_gains - own_columns(gain_update)
    return (
        text_embed,
        image_embed,
        grad_states,
        weight_grad,
        new_rows.T,
        new_cols.reshape(-1),
        new_weights,
        new_low,
        own_columns(gain_grad),
        own_columns(new_gain_stats),
        new_gains,
        to_low(new_gains),
        ratios[0],
    )


def solution(mesh):
    in_specs = (
        P(("group", "shard"), None),
        P(("group", "shard"), None),
        P(),
        P(),
        P("shard", None),
        P(None, "shard"),
        P(),
        P(("group", "shard")),
        P(None, "shard"),
        P(),
        P(None, "shard"),
    )
    out_specs = (
        P(("group", "shard"), None),
        P(("group", "shard"), None),
        P(("group", "shard"), None),
        P("shard", None),
        P(None, "shard"),
        P(),
        P("shard", None),
        P("shard", None),
        P(None, "shard"),
        P(None, "shard"),
        P(None, "shard"),
        P(None, "shard"),
        P(),
    )
    return jax.shard_map(shards, mesh=mesh, in_specs=in_specs, out_specs=out_specs, check_vma=False)
```

```python
import functools

import jax
import jax.numpy as jnp
import numpy as np
from jax import lax
from jax.experimental import pallas as pl
from jax.experimental.pallas import tpu as pltpu
from jax.sharding import PartitionSpec as P

HEADS = 12
IMG_ROWS = 50
TXT_ROWS = 16
NORM_EPSILON = 1e-06
STAT_EPSILON = 1e-30
CLIP_LEVEL = 0.1
WEIGHT_RATE = 0.4
GAIN_RATE = 5.0
GELU_SCALE = 0.7978845608028654
GELU_CUBE = 0.044715
MASKED = -1e30
IMAGES_STEP = 8
FF_STEPS = 4
ROW_STEPS = 2
TEXTS_GROUP = 5
VMEM_LIMIT = 24 * 1024 * 1024
VMEM_MORE = 48 * 1024 * 1024
VMEM_MOST = 62 * 1024 * 1024
COST_SCALE = 100


def to_low(value):
    return value.astype(jnp.bfloat16)


def wide(value):
    return value.astype(jnp.float32)


def dot(left, right):
    return jnp.dot(left, right, preferred_element_type=jnp.float32)


def dot_tn(left, right):
    return lax.dot_general(
        left, right, (((0,), (0,)), ((), ())), preferred_element_type=jnp.float32
    )


def dot_nt(left, right):
    return lax.dot_general(
        left, right, (((1,), (1,)), ((), ())), preferred_element_type=jnp.float32
    )


def iota(shape, axis):
    return lax.broadcasted_iota(jnp.int32, shape, axis)


def normalize(value):
    centred = value - jnp.mean(value, axis=-1, keepdims=True)
    inverse = lax.rsqrt(jnp.mean(centred * centred, axis=-1, keepdims=True) + NORM_EPSILON)
    return (centred * inverse, inverse)


def norm_back(grad_hat, normed, inverse):
    return inverse * (
        grad_hat
        - jnp.mean(grad_hat, axis=-1, keepdims=True)
        - normed * jnp.mean(grad_hat * normed, axis=-1, keepdims=True)
    )


def gelu(value):
    bent = jnp.tanh(GELU_SCALE * (value + GELU_CUBE * value * value * value))
    return 0.5 * value * (1.0 + bent)


def gelu_slope(value):
    inner = GELU_SCALE + (GELU_SCALE * GELU_CUBE) * (value * value)
    share = 0.5 + 0.5 * jnp.tanh(value * inner)
    result = value * share
    slope = share + (result - result * share) * (6.0 * inner - 4.0 * GELU_SCALE)
    return result, slope


def blocks_of(total, size=32):
    return [slice(start, min(start + size, total)) for start in range(0, total, size)]


def halves_mask(rows, width):
    lane = iota((rows, width), 1)
    return to_low((lane < width // 2).astype(jnp.float32))


def call(kernel, grid, in_specs, out_specs, out_shapes, scratch, args, flops, after=(), place=None, least=2e9, vmem=VMEM_LIMIT, large=()):
    moved = sum(a.size * a.dtype.itemsize for a in args)
    moved += sum(o.size * o.dtype.itemsize for o in out_shapes)
    lead = 0 if place is None else 1
    body = kernel
    if after:
        first, skipped = lead + len(args), len(after)

        def body(*refs):
            kernel(*refs[:first], *refs[first + skipped :])

    in_specs = list(in_specs) + [pl.BlockSpec(memory_space=pl.ANY)] * len(after)
    spec = dict(grid=grid, in_specs=in_specs, out_specs=out_specs, scratch_shapes=scratch)
    if place is not None:
        spec = dict(
            grid_spec=pltpu.PrefetchScalarGridSpec(num_scalar_prefetch=1, **spec)
        )
        args = (place,) + tuple(args)
    out_shapes = [
        pltpu.MemorySpace.HBM(out.shape, out.dtype) if index in large else out
        for index, out in enumerate(out_shapes)
    ]
    return pl.pallas_call(
        body,
        out_shape=out_shapes,
        compiler_params=pltpu.CompilerParams(vmem_limit_bytes=vmem),
        cost_estimate=pl.CostEstimate(
            flops=int(COST_SCALE * max(flops, least)),
            bytes_accessed=int(COST_SCALE * moved),
            transcendentals=0,
        ),
        **spec,
    )(*args, *after)


def room(images):
    return VMEM_LIMIT if images * 2 < VMEM_LIMIT // 2 else VMEM_MOST


def shape(dims, dtype=jnp.float32):
    return jax.ShapeDtypeStruct(dims, dtype)


def whole(array):
    zeros = (0,) * array.ndim
    return pl.BlockSpec(array.shape, lambda *_: zeros)


def some(array, first, count):
    return pl.BlockSpec(
        (count,) + array.shape[1:], lambda *_: (first // count,) + (0,) * (array.ndim - 1)
    )


SMEM = pl.BlockSpec(memory_space=pltpu.SMEM)


def image_attention_kernel(
    total_rows,
    x_ref, wq_ref, wk_ref, wv_ref, wo_ref, gain_ref,
    out_ref,
    rows_scr, x_scr, class_scr, query_scr, mixed_scr, low_scr,
):
    phase, step = pl.program_id(0), pl.program_id(1)
    steps = pl.num_programs(1)
    count, rows, width = rows_scr.shape
    images = IMAGES_STEP
    pairs = HEADS // 2
    pair = width // pairs

    @pl.when(phase == 0)
    def _():
        x = wide(x_ref[...])
        x = jnp.where(step * rows + iota((rows, 1), 0) < total_rows, x, 0.0)
        a = to_low(normalize(x)[0] * gain_ref[0:1, :])
        rows_scr[step] = a
        pick = iota((images, rows), 1) == iota((images, rows), 0) * IMG_ROWS
        pick = to_low(pick.astype(jnp.float32))
        class_scr[step] = dot(pick, a)
        x_scr[step] = dot(pick, to_low(x))

    @pl.when((phase == 1) & (step == 0))
    def _():
        query = to_low(dot(to_low(class_scr[...].reshape(count * images, width)), wq_ref[...]))
        first = halves_mask(count * images, pair)
        for which in range(pairs):
            lanes = slice(which * pair, (which + 1) * pair)
            for half in range(2):
                head = 2 * which + half
                own = query[:, lanes] * (first if half == 0 else 1 - first)
                query_scr[:, head * images : (head + 1) * images, :] = dot_nt(
                    own, wk_ref[:, lanes]
                ).reshape(count, images, width)

    @pl.when(phase == 1)
    def _():
        a = rows_scr[step]
        scores = dot_nt(to_low(query_scr[step]), a) * (width // HEADS) ** (-0.5)
        start = (iota(scores.shape, 0) & (images - 1)) * IMG_ROWS
        column = iota(scores.shape, 1)
        scores = jnp.where((column >= start) & (column < start + IMG_ROWS), scores, MASKED)
        power = jnp.exp(scores - jnp.max(scores, axis=-1, keepdims=True))
        probs = power / jnp.sum(power, axis=-1, keepdims=True)
        mixed_scr[step] = dot(to_low(probs), a)

    @pl.when((phase == 1) & (step == steps - 1))
    def _():
        lane = iota((count * images, pair), 1)
        for which in range(pairs):
            lanes = slice(which * pair, (which + 1) * pair)
            halves = []
            for half in range(2):
                head = 2 * which + half
                own = mixed_scr[:, head * images : (head + 1) * images, :]
                halves.append(dot(to_low(own.reshape(count * images, width)), wv_ref[:, lanes]))
            low_scr[:, lanes] = to_low(jnp.where(lane < pair // 2, halves[0], halves[1]))
        out_ref[...] = x_scr[...].reshape(count * images, width) + dot(low_scr[...], wo_ref[...])


def image_attention(states, weights, gains, after=()):
    total_rows, width = states.shape
    rows = IMAGES_STEP * IMG_ROWS
    steps = pl.cdiv(total_rows, rows)
    padded = steps * IMAGES_STEP

    def part(which):
        return pl.BlockSpec((width, width), lambda phase, step: (0, which))

    return call(
        functools.partial(image_attention_kernel, total_rows),
        (2, steps),
        [
            pl.BlockSpec(
                (rows, width), lambda phase, step: (jnp.where(phase == 0, step, steps - 1), 0)
            ),
            part(0), part(1), part(2), part(3),
            whole(gains),
        ],
        [pl.BlockSpec((padded, width), lambda phase, step: (0, 0))],
        [shape((padded, width))],
        [
            pltpu.VMEM((steps, rows, width), jnp.bfloat16),
            pltpu.VMEM((steps, IMAGES_STEP, width), jnp.float32),
            pltpu.VMEM((steps, IMAGES_STEP, width), jnp.float32),
            pltpu.VMEM((steps, HEADS * IMAGES_STEP, width), jnp.float32),
            pltpu.VMEM((steps, HEADS * IMAGES_STEP, width), jnp.float32),
            pltpu.VMEM((padded, width), jnp.bfloat16),
        ],
        (states, weights, weights, weights, weights, gains),
        4 * total_rows * width * HEADS * IMAGES_STEP * 3,
        after,
        vmem=VMEM_MORE,
    )[0]


def image_mlp_kernel(x_ref, gain_ref, up_ref, down_ref, out_ref, low_ref, norm_scr, total_scr):
    step = pl.program_id(0)

    @pl.when(step == 0)
    def _():
        norm_scr[...] = to_low(normalize(x_ref[...])[0] * gain_ref[1:2, :])
        total_scr[...] = x_ref[...]

    hidden = to_low(gelu(dot(norm_scr[...], up_ref[...])))
    total_scr[...] += dot_nt(hidden, down_ref[...])

    @pl.when(step == pl.num_programs(0) - 1)
    def _():
        result = total_scr[...]
        result = result * lax.rsqrt(
            jnp.sum(result * result, axis=-1, keepdims=True) + NORM_EPSILON
        )
        count = out_ref.shape[0]
        out_ref[...] = result[:count]
        low_ref[...] = jnp.zeros_like(low_ref)
        low_ref[: result.shape[0], :] = to_low(
            jnp.where(iota(result.shape, 0) < count, result, 0.0)
        )


def image_mlp(first, weights, gains, images, after=()):
    padded, width = first.shape
    hidden = (weights.shape[1] - 4 * width) // 2
    block = hidden // FF_STEPS
    lead = 4 * width // block
    return call(
        image_mlp_kernel,
        (FF_STEPS,),
        [
            whole(first),
            whole(gains),
            pl.BlockSpec((width, block), lambda step: (0, lead + step)),
            pl.BlockSpec((width, block), lambda step: (0, lead + FF_STEPS + step)),
        ],
        [
            pl.BlockSpec((images, width), lambda step: (0, 0)),
            pl.BlockSpec((pair_rows(padded), width), lambda step: (0, 0)),
        ],
        [shape((images, width)), shape((pair_rows(padded), width), jnp.bfloat16)],
        [pltpu.VMEM((padded, width), jnp.bfloat16), pltpu.VMEM((padded, width), jnp.float32)],
        (first, gains, weights, weights),
        4 * padded * width * hidden * 3,
        after,
        vmem=VMEM_MORE,
    )


class Place:
    def __init__(self, chips, rows, groups, stacked=False, halves=False):
        self.chips, self.rows, self.groups = chips, rows, groups
        self.stacked, self.halves = stacked, halves

    def column(self, step, group):
        if not self.halves:
            return step ^ group
        side = step & 1
        return 2 * side + (((group >> side) & 1) ^ (step >> 1))


def weight_copies(place, pos_ref, blocks, w_scr, sems):
    if place is None:
        return [[pltpu.make_async_copy(blocks[0], w_scr, sems.at[0])]]
    copies = [[] for _ in range(place.groups)]
    width = w_scr.shape[2] // place.groups
    count = 0
    for ref, lines, masks, same_core in blocks:
        for index, (line, mask) in enumerate((l, m) for m in masks for l in lines):
            core = pos_ref[1] if same_core else 1 - pos_ref[1]
            row = (pos_ref[0] ^ line) * 2 + core
            if place.stacked:
                target = w_scr.at[row * place.groups + (pos_ref[2] ^ mask)]
            else:
                column = pl.multiple_of(place.column(mask, pos_ref[2]) * width, width)
                target = w_scr.at[row, :, pl.ds(column, width)]
            copies[mask].append(pltpu.make_async_copy(ref.at[index], target, sems.at[count]))
            count += 1
    return copies


def load_weights(copies, step):
    @pl.when(step == 0)
    def _():
        for group in copies:
            for copy in group:
                copy.start()

    for mask, group in enumerate(copies):

        @pl.when(step == mask)
        def _():
            for copy in group:
                copy.wait()


class Weights:
    def __init__(self, place, arrays, keys, columns):
        self.place, self.arrays, self.keys, self.columns = place, arrays, keys, columns

    def specs(self):
        return [pl.BlockSpec(memory_space=pl.ANY)] * len(self.arrays)

    def blocks(self, refs):
        if self.place is None:
            return list(refs)
        return [(ref,) + key for ref, key in zip(refs, self.keys)]

    def scratch(self, width):
        if self.place is None:
            dims, count = self.arrays[0].shape, 1
        else:
            count = 2 * self.place.chips * self.place.groups
            shards = count if self.place.stacked else 2 * self.place.chips
            dims = (shards, self.place.rows, self.columns)
        return [pltpu.VMEM(dims, jnp.bfloat16), pltpu.SemaphoreType.DMA((count,))]

    def column(self, step, group):
        return step if self.place is None else self.place.column(step, group)

    def lanes(self, pos_ref, step, block):
        return pl.ds(pl.multiple_of(self.column(step, pos_ref[2]) * block, block), block)

    def out(self, width):
        return jax.ShapeDtypeStruct(self.scratch(width)[0].shape, jnp.bfloat16)


def rows_of(ref, lanes):
    value = ref[:, :, lanes]
    return value.reshape(value.shape[0] * value.shape[1], value.shape[2])


GROUP = 4 * TXT_ROWS


def group_bias(width):
    key = lax.shift_right_logical(iota((GROUP, width), 0), 4)
    query = lax.shift_right_logical(iota((GROUP, width), 1) & (GROUP - 1), 4)
    return jnp.where(key == query, 0.0, MASKED)


def group_softmax(scores, bias):
    scores = scores + bias
    power = jnp.exp(scores - jnp.max(scores, axis=0, keepdims=True))
    return power * (1.0 / jnp.sum(power, axis=0, keepdims=True))


def both_heads(value, first, second):
    return jnp.concatenate([value * first, value * second], axis=0)


def group_rows(rows):
    for start in range(0, rows, GROUP):
        start = min(start, rows - GROUP)
        yield slice(start, start + GROUP)


def project_kernel(weights, count, pos_ref, x_ref, gain_ref, *refs):
    block_refs, refs = refs[:count], refs[count:]
    qkv_ref, w_out_ref, norm_scr, w_scr, sems, out_sem = refs
    width = x_ref.shape[1]
    step = pl.program_id(0)
    copies = weight_copies(weights.place, pos_ref, weights.blocks(block_refs), w_scr, sems)
    copy_out = pltpu.make_async_copy(w_scr, w_out_ref, out_sem)
    load_weights(copies, step)

    @pl.when(step == 0)
    def _():
        norm_scr[...] = to_low(normalize(wide(x_ref[...]))[0] * gain_ref[0:1, :])

    @pl.when(step == pl.num_programs(0) - 1)
    def _():
        copy_out.start()

    @pl.when(weights.column(step, pos_ref[2]) < 3)
    def _():
        w = rows_of(w_scr, weights.lanes(pos_ref, step, width))
        products = [dot(norm_scr[...], w[:, lanes]) for lanes in blocks_of(width, COLUMN_CHUNK)]
        for lanes, product in zip(blocks_of(width, COLUMN_CHUNK), products):
            qkv_ref[:, lanes] = to_low(product)

    @pl.when(step == pl.num_programs(0) - 1)
    def _():
        copy_out.wait()


def project(states, weights, gains, pos, after=()):
    total, width = states.shape
    qkv, full = call(
        functools.partial(project_kernel, weights, len(weights.arrays)),
        (4,),
        [whole(states), whole(gains)] + weights.specs(),
        [
            pl.BlockSpec((total, width), lambda step, pos: (0, weights.column(step, pos[2]))),
            pl.BlockSpec(memory_space=pl.ANY),
        ],
        [shape((total, 4 * width), jnp.bfloat16), weights.out(width)],
        [pltpu.VMEM((total, width), jnp.bfloat16)]
        + weights.scratch(width)
        + [pltpu.SemaphoreType.DMA],
        (states, gains, *weights.arrays),
        6 * total * width * width * 1.5,
        after,
        pos,
        large=(1,),
    )
    return qkv, full.reshape(width, -1)


def attention_forward_kernel(x_ref, qkv_ref, w_ref, mixed_ref, out_ref):
    rows, width = x_ref.shape
    pairs = HEADS // 2
    pair = width // pairs
    scale = (width // HEADS) ** (-0.5)
    first = halves_mask(GROUP, pair)
    second = 1 - first
    first_scaled, second_scaled = first * scale, second * scale
    bias = group_bias(width)
    lane = iota((GROUP, pair), 1)

    def part(here, which, kind):
        start = kind * width + which * pair
        return qkv_ref[here, start : start + pair]

    def scores_of(here):
        scores = [
            dot_nt(
                part(here, which, 1), both_heads(part(here, which, 0), first_scaled, second_scaled)
            )
            for which in range(pairs)
        ]
        return jnp.concatenate(scores, axis=1)

    groups = list(group_rows(rows))
    scores = scores_of(groups[0])
    for index, here in enumerate(groups):
        following = scores_of(groups[index + 1]) if index + 1 < len(groups) else None
        probs = to_low(group_softmax(scores, bias))
        both = [
            dot_tn(probs[:, which * pair : (which + 1) * pair], part(here, which, 2))
            for which in range(pairs)
        ]
        for which in range(pairs):
            mixed_ref[here, which * pair : (which + 1) * pair] = to_low(
                jnp.where(lane < pair // 2, both[which][:GROUP], both[which][GROUP:])
            )
        scores = following
    out_ref[...] = wide(x_ref[...]) + dot(mixed_ref[...], w_ref[...])


def attention_forward(states, qkv, weights, after=()):
    total, width = states.shape
    rows = total // ROW_STEPS

    def by_rows(columns):
        return pl.BlockSpec((rows, columns), lambda step: (step, 0))

    return call(
        attention_forward_kernel,
        (ROW_STEPS,),
        [by_rows(width), by_rows(3 * width), pl.BlockSpec((width, width), lambda step: (0, 3))],
        [by_rows(width), by_rows(width)],
        [shape((total, width), jnp.bfloat16), shape((total, width))],
        [],
        (states, qkv, weights),
        6 * total * width * width * 1.5,
        after,
    )


def split_low(value):
    high = to_low(value)
    return high, to_low(value - wide(high))


def pair_rows(texts):
    return -(-texts // 16) * 16


def store_pair(ref, texts, high, low):
    half = pair_rows(texts)
    ref[...] = jnp.zeros_like(ref)
    ref[:texts, :] = high
    ref[half : half + texts, :] = low


COLUMN_CHUNK = 256


def up_kernel(weights, count, pos_ref, x_ref, gain_ref, *refs):
    block_refs, refs = refs[:count], refs[count:]
    hidden_ref, slope_ref, pooled_ref, w_out_ref, norm_scr, low_scr, w_scr, sems, out_sem = refs
    total, width = x_ref.shape
    texts = total // TXT_ROWS
    block = hidden_ref.shape[1]
    step = pl.program_id(0)
    last = pl.num_programs(0) - 1
    copies = weight_copies(weights.place, pos_ref, weights.blocks(block_refs), w_scr, sems)
    copy_out = pltpu.make_async_copy(w_scr, w_out_ref, out_sem)
    load_weights(copies, step)

    @pl.when(step == 0)
    def _():
        x = x_ref[...]
        norm_scr[...] = to_low(normalize(x)[0] * gain_ref[1:2, :])
        pooled_ref[...] = jnp.sum(x.reshape(texts, TXT_ROWS, width), axis=1)

    @pl.when(step == last)
    def _():
        copy_out.start()

    w = rows_of(w_scr, weights.lanes(pos_ref, step, block))
    pool = lax.shift_right_logical(iota((texts, total), 1), 4) == iota((texts, total), 0)
    pool = to_low(pool.astype(jnp.float32))
    chunks = blocks_of(block, COLUMN_CHUNK)
    product = dot(norm_scr[...], w[:, chunks[0]])
    for index, lanes in enumerate(chunks):
        following = None
        if index + 1 < len(chunks):
            following = dot(norm_scr[...], w[:, chunks[index + 1]])
        value, slope = gelu_slope(product)
        slope_ref[:, lanes] = to_low(slope)
        low_scr[:, lanes] = to_low(value)
        product = following
    store_pair(hidden_ref, texts, *split_low(dot(pool, low_scr[...])))

    @pl.when(step == last)
    def _():
        copy_out.wait()


def up_forward(states, weights, gains, pos, after=()):
    total, width = states.shape
    hidden = weights.columns
    block = hidden // FF_STEPS
    texts = total // TXT_ROWS
    columns = lambda step, pos: (0, weights.column(step, pos[2]))
    hidden_sum, slope, pooled, full = call(
        functools.partial(up_kernel, weights, len(weights.arrays)),
        (FF_STEPS,),
        [whole(states), whole(gains)] + weights.specs(),
        [
            pl.BlockSpec((2 * pair_rows(texts), block), columns),
            pl.BlockSpec((total, block), columns),
            pl.BlockSpec((texts, width), lambda step, pos: (0, 0)),
            pl.BlockSpec(memory_space=pl.ANY),
        ],
        [
            shape((2 * pair_rows(texts), hidden), jnp.bfloat16),
            shape((total, hidden), jnp.bfloat16), shape((texts, width)),
            weights.out(width),
        ],
        [pltpu.VMEM((total, width), jnp.bfloat16), pltpu.VMEM((total, block), jnp.bfloat16)]
        + weights.scratch(width)
        + [pltpu.SemaphoreType.DMA],
        (states, gains, *weights.arrays),
        2 * total * width * hidden * 1.5,
        after,
        pos,
        large=(1, 3),
    )
    return hidden_sum, slope, pooled, full.reshape(width, -1)


def scores_kernel(
    weights, count, images, image_count, pos_ref,
    hidden_ref, pooled_ref, bias_ref, scale_ref, *refs,
):
    block_refs, refs = refs[:count], refs[count:]
    image_refs, refs = refs[:image_count], refs[image_count:]
    embed_ref, inverse_ref, scores_ref, row_ref, col_ref, w_out_ref, image_out_ref = refs[:7]
    total_scr, w_scr, sems, out_sem, image_scr, image_sems, image_out_sem = refs[7:]
    step = pl.program_id(0)
    last = pl.num_programs(0) - 1
    texts = embed_ref.shape[0]
    half = pair_rows(texts)
    copies = weight_copies(weights.place, pos_ref, weights.blocks(block_refs), w_scr, sems)
    copy_out = pltpu.make_async_copy(w_scr, w_out_ref, out_sem)
    image_copies = weight_copies(
        images.place, pos_ref, images.blocks(image_refs), image_scr, image_sems
    )
    image_out = pltpu.make_async_copy(image_scr, image_out_ref, image_out_sem)
    load_weights(copies, step)

    @pl.when(step == 0)
    def _():
        total_scr[...] = pooled_ref[...]
        for group in image_copies:
            for copy in group:
                copy.start()

    @pl.when(step == last)
    def _():
        copy_out.start()

    w = rows_of(w_scr, weights.lanes(pos_ref, step, hidden_ref.shape[1]))
    both = dot_nt(hidden_ref[...], w)
    total_scr[...] += both[:texts] + both[half : half + texts]

    @pl.when(step == last)
    def _():
        for group in image_copies:
            for copy in group:
                copy.wait()
        image_out.start()
        pooled = total_scr[...] * (1.0 / TXT_ROWS)
        inverse = lax.rsqrt(jnp.sum(pooled * pooled, axis=-1, keepdims=True) + NORM_EPSILON)
        embed = pooled * inverse
        embed_ref[...] = embed
        inverse_ref[...] = inverse
        all_image = rows_of(image_scr, slice(0, image_scr.shape[2]))
        scores = scale_ref[0, 0] * dot_nt(to_low(embed), all_image) + bias_ref[...]
        scores_ref[...] = scores
        top = jnp.max(scores, axis=1, keepdims=True)
        row_ref[...] = top + jnp.log(jnp.sum(jnp.exp(scores - top), axis=1, keepdims=True))
        top = jnp.max(scores, axis=0, keepdims=True)
        col_ref[...] = top + jnp.log(jnp.sum(jnp.exp(scores - top), axis=0, keepdims=True))
        copy_out.wait()
        image_out.wait()


def scores_forward(hidden, pooled, weights, images, bias, scale, pos, after=()):
    texts, width = pooled.shape
    total = hidden.shape[1]
    block = total // FF_STEPS
    count = bias.shape[1]
    outs = [
        shape((texts, width)), shape((texts, 1)), shape((texts, count)),
        shape((texts, 1)), shape((1, count)),
    ]
    *results, full, full_images = call(
        functools.partial(
            scores_kernel, weights, len(weights.arrays), images, len(images.arrays)
        ),
        (FF_STEPS,),
        [
            pl.BlockSpec(
                (hidden.shape[0], block), lambda step, pos: (0, weights.column(step, pos[2]))
            ),
            whole(pooled), whole(bias), SMEM,
        ]
        + weights.specs()
        + images.specs(),
        [whole(out) for out in outs] + [pl.BlockSpec(memory_space=pl.ANY)] * 2,
        outs + [weights.out(width), images.out(width)],
        [pltpu.VMEM((texts, width), jnp.float32)]
        + weights.scratch(width)
        + [pltpu.SemaphoreType.DMA]
        + images.scratch(width)
        + [pltpu.SemaphoreType.DMA],
        (hidden, pooled, bias, scale, *weights.arrays, *images.arrays),
        2 * texts * width * (2 * total + count) * 3,
        after,
        pos,
        vmem=room(count * width),
        large=(5, 6),
    )
    return *results, full.reshape(width, -1), full_images.reshape(count, width)


class Split:
    def __init__(self, place, width, columns, lines_first=False):
        self.place, self.width, self.columns = place, width, columns
        self.lines_first = lines_first

    def specs(self):
        if self.place is None:
            return [pl.BlockSpec((self.width, self.columns), lambda step, pos: (0, step))]
        tail = (self.place.rows, self.columns)
        if self.lines_first:
            block = (self.place.chips, 1) + tail
            return [pl.BlockSpec(block, lambda step, pos: (0, step ^ pos[2], 0, 0))] * 2
        block = (1, self.place.chips) + tail
        return [pl.BlockSpec(block, lambda step, pos: (step ^ pos[2], 0, 0, 0))] * 2

    def outs(self, steps):
        if self.place is None:
            return [shape((self.width, steps * self.columns), jnp.bfloat16)]
        lead = (self.place.chips, steps) if self.lines_first else (steps, self.place.chips)
        return [shape(lead + (self.place.rows, self.columns), jnp.bfloat16)] * 2

    def scratch(self):
        if self.place is None:
            return []
        return [
            pltpu.VMEM((2 * self.place.chips, self.place.rows, self.columns), jnp.bfloat16)
        ]

    def store(self, value, refs, scr, pos_ref):
        if self.place is None:
            refs[0][...] = to_low(value)
            return
        scr[0][...] = to_low(value).reshape(scr[0].shape)
        for line in range(self.place.chips):
            row = (pos_ref[0] ^ line) * 2
            at = (line, 0) if self.lines_first else (0, line)
            refs[0][at] = scr[0][row + pos_ref[1]]
            refs[1][at] = scr[0][row + 1 - pos_ref[1]]


def scores_backward_kernel(
    split, pos_ref,
    scores_ref, row_ref, col_ref, target_ref, scale_ref, image_ref, embed_ref, inverse_ref,
    hidden_ref, w_ref,
    grad_hidden_ref, grad_out_ref, *refs,
):
    count = len(split.specs())
    grad_refs, low_scr, scr = refs[:count], refs[count], refs[count + 1 :]

    @pl.when(pl.program_id(0) == 0)
    def _():
        scores = scores_ref[...]
        hit = (iota(scores.shape, 1) == target_ref[...]).astype(jnp.float32)
        grad = scale_ref[0, 0] * (
            0.5 * (jnp.exp(scores - row_ref[...]) + jnp.exp(scores - col_ref[...])) - hit
        )
        grad_text = dot(to_low(grad), image_ref[...])
        embed = embed_ref[...]
        grad_pooled = inverse_ref[...] * (
            grad_text - embed * jnp.sum(embed * grad_text, axis=-1, keepdims=True)
        )
        grad_out = grad_pooled * (1.0 / TXT_ROWS)
        grad_out_ref[...] = grad_out
        store_pair(low_scr, grad_out.shape[0], to_low(grad_out), to_low(grad_out))

    branch = low_scr[...]
    grad_hidden_ref[...] = dot(branch[: grad_hidden_ref.shape[0]], w_ref[...])
    split.store(dot_tn(branch, hidden_ref[...]), grad_refs, scr, pos_ref)


def scores_backward(
    scores, row, col, target, scale, images, embed, inverse, hidden, weights, place, pos, after=()
):
    texts, width = embed.shape
    total = hidden.shape[1]
    block = total // FF_STEPS
    split = Split(place, width, block)
    columns = lambda step, pos: (0, step)
    grad_hidden, grad_out, *grads = call(
        functools.partial(scores_backward_kernel, split),
        (FF_STEPS,),
        [
            whole(scores), whole(row), whole(col), whole(target), SMEM, whole(images),
            whole(embed), whole(inverse),
            pl.BlockSpec((hidden.shape[0], block), columns),
            pl.BlockSpec((width, block), columns),
        ],
        [
            pl.BlockSpec((texts, block), columns),
            pl.BlockSpec((texts, width), lambda step, pos: (0, 0)),
        ]
        + split.specs(),
        [shape((texts, total)), shape((texts, width))] + split.outs(FF_STEPS),
        [pltpu.VMEM((hidden.shape[0], width), jnp.bfloat16)] + split.scratch(),
        (scores, row, col, target, scale, images, embed, inverse, hidden, weights),
        2 * texts * width * (3 * total + scores.shape[1]) * 3,
        after,
        pos,
        vmem=room(images.size),
        large=(2, 3),
    )
    return grad_hidden, grad_out, grads


def turned_norm_kernel(which, x_ref, gain_ref, out_ref):
    out_ref[...] = to_low(normalize(wide(x_ref[...]))[0] * gain_ref[which : which + 1, :]).T


def turned_norm(states, gains, which, after=()):
    total, width = states.shape
    return call(
        functools.partial(turned_norm_kernel, which),
        (1,),
        [whole(states), whole(gains)],
        [pl.BlockSpec((width, total), lambda step: (0, 0))],
        [shape((width, total), jnp.bfloat16)],
        [],
        (states, gains),
        10 * total * width,
        after,
    )[0]


def up_backward_kernel(split, pos_ref, grad_ref, slope_ref, norm_ref, w_ref, grad_x_ref, *refs):
    count = len(split.specs())
    grad_refs, scr = refs[:count], refs[count:]
    texts, block = grad_ref.shape
    total = slope_ref.shape[0]

    @pl.when(pl.program_id(0) == 0)
    def _():
        grad_x_ref[...] = jnp.zeros_like(grad_x_ref)

    spread = jnp.broadcast_to(grad_ref[...][:, None, :], (texts, TXT_ROWS, block))
    grad = to_low(spread.reshape(total, block) * wide(slope_ref[...]))
    grad_w = dot(norm_ref[...], grad)
    grad_x = dot_nt(grad, w_ref[...])
    split.store(grad_w, grad_refs, scr, pos_ref)
    grad_x_ref[...] += grad_x


def up_backward(grad_hidden, slope, norm, weights, place, pos, after=()):
    width, total = norm.shape
    texts, hidden = grad_hidden.shape
    block = hidden // FF_STEPS
    split = Split(place, width, block)
    columns = lambda step, pos: (0, step)
    grad_x, *grads = call(
        functools.partial(up_backward_kernel, split),
        (FF_STEPS,),
        [
            pl.BlockSpec((texts, block), columns),
            pl.BlockSpec((total, block), columns),
            whole(norm),
            pl.BlockSpec((width, block), columns),
        ],
        [pl.BlockSpec((total, width), lambda step, pos: (0, 0))] + split.specs(),
        [shape((total, width))] + split.outs(FF_STEPS),
        split.scratch(),
        (grad_hidden, slope, norm, weights),
        4 * total * width * hidden * 1.5,
        after,
        pos,
        large=(1, 2),
    )
    return grad_x, grads


def first_backward_kernel(
    grad_b_ref, grad_out_ref, x_ref, gain_ref, w_ref,
    grad_x_ref, grad_low_ref, grad_mixed_ref, grad_gain_ref,
):
    rows, width = x_ref.shape
    texts = rows // TXT_ROWS
    hat, inverse = normalize(x_ref[...])
    grad_b = grad_b_ref[...]
    grad_gain = jnp.sum(grad_b * hat, axis=0, keepdims=True)
    spread = jnp.broadcast_to(grad_out_ref[...].reshape(texts, 1, width), (texts, TXT_ROWS, width))
    grad_x = spread.reshape(rows, width) + norm_back(grad_b * gain_ref[1:2, :], hat, inverse)
    grad_x_ref[...] = grad_x
    grad_low = to_low(grad_x)
    grad_low_ref[...] = grad_low
    grad_mixed_ref[...] = to_low(dot_nt(grad_low, w_ref[...]))

    @pl.when(pl.program_id(0) == 0)
    def _():
        grad_gain_ref[...] = grad_gain

    @pl.when(pl.program_id(0) > 0)
    def _():
        grad_gain_ref[...] += grad_gain


def first_backward(grad_b, grad_out, states, gains, weights, after=()):
    total, width = states.shape
    rows = total // ROW_STEPS
    texts = rows // TXT_ROWS
    by_rows = pl.BlockSpec((rows, width), lambda step: (step, 0))
    return call(
        first_backward_kernel,
        (ROW_STEPS,),
        [
            by_rows,
            pl.BlockSpec((1, texts, width), lambda step: (step, 0, 0)),
            by_rows,
            whole(gains),
            pl.BlockSpec((width, width), lambda step: (0, 3)),
        ],
        [by_rows, by_rows, by_rows, pl.BlockSpec((1, width), lambda step: (0, 0))],
        [
            shape((total, width)),
            shape((total, width), jnp.bfloat16),
            shape((total, width), jnp.bfloat16),
            shape((1, width)),
        ],
        [],
        (grad_b, grad_out.reshape(ROW_STEPS, texts, width), states, gains, weights),
        2 * total * width * width * 1.5,
        after,
    )


def attention_backward_kernel(qkv_ref, grad_ref, grad_qkv_ref):
    rows, width = grad_ref.shape
    pairs = HEADS // 2
    pair = width // pairs
    scale = (width // HEADS) ** (-0.5)
    first = halves_mask(GROUP, pair)
    second = 1 - first
    first_scaled, second_scaled = first * scale, second * scale
    bias = group_bias(width)
    lane = iota((GROUP, pair), 1)

    def part(here, which, kind):
        start = kind * width + which * pair
        return qkv_ref[here, start : start + pair]

    def products_of(here):
        queries = [
            both_heads(part(here, which, 0), first_scaled, second_scaled) for which in range(pairs)
        ]
        grads = [
            both_heads(grad_ref[here, which * pair : (which + 1) * pair], first, second)
            for which in range(pairs)
        ]
        scores = [dot_nt(part(here, which, 1), queries[which]) for which in range(pairs)]
        grad_probs = [dot_nt(part(here, which, 2), grads[which]) for which in range(pairs)]
        keys = [part(here, which, 1) for which in range(pairs)]
        return (
            queries, grads, keys, jnp.concatenate(scores, axis=1),
            jnp.concatenate(grad_probs, axis=1),
        )

    groups = list(group_rows(rows))
    products = products_of(groups[0])
    for index, here in enumerate(groups):
        queries, grads, keys, scores, grad_probs = products
        if index + 1 < len(groups):
            products = products_of(groups[index + 1])
        probs = group_softmax(scores, bias)
        inner = jnp.sum(probs * grad_probs, axis=0, keepdims=True)
        grad_scores = to_low(probs * (grad_probs - inner))
        probs = to_low(probs)
        results = []
        for which in range(pairs):
            lanes = slice(which * pair, (which + 1) * pair)
            own = grad_scores[:, lanes]
            both = dot_tn(own, keys[which]) * scale
            results.append((
                jnp.where(lane < pair // 2, both[:GROUP], both[GROUP:]),
                dot(own, queries[which]),
                dot(probs[:, lanes], grads[which]),
            ))
        for which in range(pairs):
            for kind in range(3):
                start = kind * width + which * pair
                grad_qkv_ref[here, start : start + pair] = to_low(results[which][kind])


def attention_backward(qkv, grad, after=()):
    total, width = grad.shape
    rows = total // ROW_STEPS

    def by_rows(columns):
        return pl.BlockSpec((rows, columns), lambda step: (step, 0))

    return call(
        attention_backward_kernel,
        (ROW_STEPS,),
        [by_rows(3 * width), by_rows(width)],
        [by_rows(3 * width)],
        [shape((total, 3 * width), jnp.bfloat16)],
        [],
        (qkv, grad),
        total * width * width * 8,
        after,
    )[0]


def first_weight_kernel(split, pos_ref, norm_ref, mixed_ref, low_ref, grad_ref, *refs):
    count = len(split.specs())
    grad_refs, scr = refs[:count], refs[count:]
    step = pl.program_id(0)

    @pl.when(step < 3)
    def _():
        split.store(dot(norm_ref[...], grad_ref[...]), grad_refs, scr, pos_ref)

    @pl.when(step == 3)
    def _():
        split.store(dot_tn(mixed_ref[...], low_ref[...]), grad_refs, scr, pos_ref)


def first_weight(norm, mixed, low, grad, place, pos, after=()):
    width, total = norm.shape
    split = Split(place, width, width)
    return call(
        functools.partial(first_weight_kernel, split),
        (4,),
        [
            whole(norm), whole(mixed), whole(low),
            pl.BlockSpec((total, width), lambda step, pos: (0, jnp.minimum(step, 2))),
        ],
        split.specs(),
        split.outs(4),
        split.scratch(),
        (norm, mixed, low, grad),
        8 * total * width * width * 1.5,
        after,
        pos,
        large=(0, 1),
    )


def states_backward_kernel(grad_ref, grad_x_ref, x_ref, gain_ref, w_ref, out_ref, grad_gain_ref):
    parts = blocks_of(x_ref.shape[0], 208)
    grads = [dot_nt(grad_ref[here, :], w_ref[...]) for here in parts]
    results = []
    grad_gain = 0.0
    for here, grad_a in zip(parts, grads):
        hat, inverse = normalize(wide(x_ref[here, :]))
        grad_gain = grad_gain + jnp.sum(grad_a * hat, axis=0, keepdims=True)
        results.append(
            grad_x_ref[here, :] + norm_back(grad_a * gain_ref[0:1, :], hat, inverse)
        )
    for here, result in zip(parts, results):
        out_ref[here, :] = result

    @pl.when(pl.program_id(0) == 0)
    def _():
        grad_gain_ref[...] = grad_gain

    @pl.when(pl.program_id(0) > 0)
    def _():
        grad_gain_ref[...] += grad_gain


def states_backward(grad, grad_x, states, gains, weights, after=()):
    total, width = states.shape
    rows = total // ROW_STEPS

    def by_rows(columns):
        return pl.BlockSpec((rows, columns), lambda step: (step, 0))

    return call(
        states_backward_kernel,
        (ROW_STEPS,),
        [
            by_rows(3 * width),
            by_rows(width),
            by_rows(width),
            whole(gains),
            pl.BlockSpec((width, 3 * width), lambda step: (0, 0)),
        ],
        [by_rows(width), pl.BlockSpec((1, width), lambda step: (0, 0))],
        [shape((total, width)), shape((1, width))],
        [],
        (grad, grad_x, states, gains, weights),
        6 * total * width * width * 1.5,
        after,
    )


def stats_kernel(place, edges, pos_ref, stats_ref, gain_ref, *refs):
    count = 3 if place is None else 3 * place.groups
    grad_refs, refs = refs[:count], refs[count:]
    full_ref, new_rows_ref, sums_ref = refs
    blocks = edges[-1]
    width = full_ref.shape[1] // blocks
    piece = full_ref.shape[1] // 3
    for which in range(3):
        if place is None:
            full_ref[:, which * piece : (which + 1) * piece] = wide(grad_refs[which][0])
            continue
        for mask in range(place.groups):
            part = piece // place.groups
            column = pl.multiple_of(which * piece + (pos_ref[2] ^ mask) * part, part)
            full_ref[:, pl.ds(column, part)] = wide(
                grad_refs[which * place.groups + mask][0, : full_ref.shape[0]]
            )
    sums_ref[...] = jnp.zeros_like(sums_ref)
    lane = iota((1, width), 1)
    tail = jnp.zeros((1, width), jnp.float32)
    for which in range(4):
        lower, upper = edges[which], edges[which + 1]
        total = 0.0
        for block in range(lower, upper):
            part = full_ref[:, block * width : (block + 1) * width]
            squares = part * part + STAT_EPSILON
            sums_ref[block : block + 1, :] = jnp.sum(squares, axis=0, keepdims=True)
            total = total + jnp.sum(squares, axis=1, keepdims=True)
        mean = total * (1.0 / ((upper - lower) * width))
        rows = 0.5 * stats_ref[:, which : which + 1] + 0.5 * mean
        new_rows_ref[:, which : which + 1] = rows
        tail = jnp.where(lane == which, jnp.sum(rows, axis=0, keepdims=True), tail)
        inverse = 1.0 / rows
        for block in range(lower, upper):
            part = full_ref[:, block * width : (block + 1) * width]
            sums_ref[blocks + block : blocks + block + 1, :] = jnp.sum(
                part * part * inverse, axis=0, keepdims=True
            )
    sums_ref[2 * blocks : 2 * blocks + 1, :] = tail
    if place is None:
        gain = gain_ref[...]
    else:
        terms = [wide(ref[0, full_ref.shape[0] :]) for ref in grad_refs[: place.groups]]
        terms = (terms[0] + terms[1]) + (terms[2] + terms[3])
        gain = terms[0:2] + terms[2:4] + terms[4:6]
    sums_ref[2 * blocks + 1 : 2 * blocks + 3, :] = gain


def gradient_stats(grads, stats, gain_grad, bounds, place, pos, after=()):
    rows = stats.shape[1]
    width = bounds[2] - bounds[1]
    edges = tuple(bound // width for bound in bounds)
    outs = [
        shape((rows, bounds[-1])), shape((rows, 4)),
        shape((-(-(2 * edges[-1] + 3) // 8) * 8, width)),
    ]
    args = (stats.T, gain_grad, *(array for array, _ in grads))
    return call(
        functools.partial(stats_kernel, place, edges),
        (1,),
        [whole(arg) for arg in args[:2]] + [some(array, at, 1) for array, at in grads],
        [whole(out) for out in outs],
        outs,
        [],
        args,
        10 * rows * bounds[-1],
        after,
        pos,
    )


def update_kernel(
    edges, sums_ref, old_cols_ref, rows_ref, gain_stats_ref,
    grad_ref, old_ref,
    new_ref, low_ref, new_cols_ref, ratio_ref, gain_ref, new_gain_stats_ref, gain_update_ref,
    factor_scr, cols_scr,
):
    step = pl.program_id(0)
    blocks = edges[-1]
    width = sums_ref.shape[1]
    per_step = new_ref.shape[1] // width

    @pl.when(step == 0)
    def _():
        new_cols = 0.5 * old_cols_ref[...] + 0.5 * (sums_ref[:blocks, :] * (1.0 / width))
        new_cols_ref[...] = new_cols
        cols_scr[...] = lax.rsqrt(new_cols)
        scaled = sums_ref[blocks : 2 * blocks, :] / new_cols
        lane = iota((1, ratio_ref.shape[1]), 1)
        ratios = jnp.zeros(ratio_ref.shape, jnp.float32)
        for which in range(4):
            lower, upper = edges[which], edges[which + 1]
            mean = sums_ref[2 * blocks : 2 * blocks + 1, which : which + 1] * (1.0 / width)
            total = jnp.sum(jnp.sum(scaled[lower:upper], axis=0, keepdims=True), axis=1, keepdims=True)
            total = total * mean * (1.0 / (width * width * (upper - lower)))
            ratio = jnp.maximum(1.0, jnp.sqrt(total) / CLIP_LEVEL)
            ratios = jnp.where(lane == which, ratio, ratios)
            factor = (WEIGHT_RATE / ratio) * lax.rsqrt(rows_ref[:, which : which + 1] / mean)
            for block in range(lower, upper):
                factor_scr[block] = factor
        gain = sums_ref[2 * blocks + 1 : 2 * blocks + 3, :]
        gain_ref[...] = gain
        new_stats = 0.5 * gain_stats_ref[...] + 0.5 * (gain * gain + STAT_EPSILON)
        new_gain_stats_ref[...] = new_stats
        update = gain * lax.rsqrt(new_stats)
        total = jnp.sum(update * update, axis=1, keepdims=True) * (1.0 / width)
        gain_ratios = jnp.maximum(1.0, jnp.sqrt(total) / CLIP_LEVEL)
        gain_update_ref[...] = GAIN_RATE * update / gain_ratios
        for which in range(2):
            ratios = jnp.where(lane == 4 + which, gain_ratios[which : which + 1, :], ratios)
        ratio_ref[...] = ratios

    for block in range(per_step):
        lanes = slice(block * width, (block + 1) * width)
        index = step * per_step + block
        scale = cols_scr[pl.ds(index, 1), :]
        new = old_ref[:, lanes] - grad_ref[:, lanes] * scale * factor_scr[index]
        new_ref[:, lanes] = new
        low_ref[:, lanes] = to_low(new)


def update_weights(grad, old, sums, old_cols, new_rows, gain_stats, bounds, after=()):
    rows, total = grad.shape
    width = bounds[2] - bounds[1]
    edges = tuple(bound // width for bound in bounds)
    steps = 3
    args = (sums, old_cols.reshape(-1, width), new_rows, gain_stats)
    outs = [
        shape((rows, total)), shape((rows, total), jnp.bfloat16),
        shape((edges[-1], width)), shape((1, 6)),
    ] + [shape(gain_stats.shape)] * 3
    by_columns = pl.BlockSpec((rows, total // steps), lambda step: (0, step))
    return call(
        functools.partial(update_kernel, edges),
        (steps,),
        [whole(arg) for arg in args] + [by_columns, by_columns],
        [by_columns, by_columns] + [whole(out) for out in outs[2:]],
        outs,
        [
            pltpu.VMEM((edges[-1], rows, 1), jnp.float32),
            pltpu.VMEM((edges[-1], width), jnp.float32),
        ],
        (*args, grad, old),
        10 * rows * total,
        after,
    )


def cut_kernel(counts, pos_ref, *refs):
    at = 0
    for count, out in zip(counts, refs[sum(counts) :]):
        for index in range(count):
            out[index] = to_low(refs[at + index][...])
        at += count


def cut(weights, groups, width, pos):
    rows = weights.shape[0]
    counts = (1, 2, 2)
    places = [lambda group: group]
    for piece in (1, 2):
        for side in (0, 1):
            places.append(
                lambda group, piece=piece, side=side: piece * groups
                + 2 * side
                + ((group >> side) & 1)
            )
    outs = [shape((count, rows, width), jnp.bfloat16) for count in counts]
    return call(
        functools.partial(cut_kernel, counts),
        (1,),
        [
            pl.BlockSpec((rows, width), lambda step, pos, at=at: (0, at(pos[2])))
            for at in places
        ],
        [whole(a) for a in outs],
        outs,
        [],
        (weights,) * len(places),
        len(places) * rows * width,
        (),
        pos,
        vmem=VMEM_MOST,
    )


def line_gather(own, chips):
    return [own] + [swap(own, "shard", 2 * mask) for mask in range(1, chips)]


def arrange_kernel(plan, count, *refs):
    for parts, out in zip(plan, refs[count:]):
        at = 0
        for which, start, stop in parts:
            out[at : at + stop - start] = refs[which][start:stop]
            at += stop - start


def arrange(plan, args, after=()):
    outs = [
        shape((sum(stop - start for _, start, stop in parts),) + args[parts[0][0]].shape[1:],
              args[parts[0][0]].dtype)
        for parts in plan
    ]
    return call(
        functools.partial(arrange_kernel, plan, len(args)),
        (1,),
        [whole(a) for a in args],
        [whole(a) for a in outs],
        outs,
        [],
        args,
        sum(a.size for a in outs),
        after,
        least=0,
    )


class Gather:
    def __init__(self, place, lines, quarters, columns):
        halves = len(quarters) == 2
        self.place = Place(place.chips, place.rows, place.groups, halves=halves)
        self.lines, self.columns = lines, columns
        self.blocks = list(quarters)
        if halves:
            self.blocks += [swap(quarter, "group", k + 1) for k, quarter in enumerate(quarters)]
        else:
            self.blocks += [swap(quarters[0], "group", mask) for mask in range(1, place.groups)]

    def weights(self, joined):
        masks = tuple(range(self.place.groups))
        keys = [(self.lines, (mask,), True) for mask in masks] + [(self.lines, masks, False)]
        return Weights(
            self.place, self.blocks + [in_hbm(swap(joined, "shard", 1))], keys, self.columns
        )


class RelayGather:
    def __init__(self, place, lines, quarter, columns):
        self.place, self.lines, self.columns = place, lines, columns
        self.blocks = [quarter] + [swap(quarter, "group", mask) for mask in (1, 2)]

    def plan(self):
        count = self.place.chips
        return [
            [(1, 0, count // 2)],
            [(2, count // 2, count)],
            [(0, 0, count), (1, 0, count), (2, 0, count)],
        ]

    def send_far(self, far_x, far_y, joined):
        self.far = [swap(far_x, "group", 2), swap(far_y, "group", 1)]
        self.joined = in_hbm(swap(joined, "shard", 1))

    def weights(self, corner):
        lines, half = self.lines, self.place.chips // 2
        arrays = self.blocks + self.far + [self.joined, swap(corner, "shard", 1)]
        keys = [(lines, (mask,), True) for mask in (0, 1, 2)]
        keys += [(lines[:half], (3,), True), (lines[half:], (3,), True)]
        keys += [(lines, (0, 1, 2), False), (lines, (3,), False)]
        return Weights(self.place, arrays, keys, self.columns)


def swap_blocks(blocks):
    return [swap(block, "shard", 2 * mask) for mask, block in enumerate(blocks, 1)]


def add_blocks(out, at, parts):
    total = 0.0
    for ref, place in parts:
        total = total + wide(ref[place + (Ellipsis,)])
    out[at + (Ellipsis,)] = total.astype(out.dtype)


def plane_blocks_kernel(*refs):
    count = len(refs) // 3
    for mine_ref, theirs_ref, out in zip(refs[:count], refs[count:], refs[2 * count :]):
        out[...] = to_low(wide(mine_ref[0]) + wide(theirs_ref[0]))


def far_kernel(mine_ref, theirs_ref, first_ref, second_ref):
    half = first_ref.shape[0]
    for line in range(2 * half):
        out = first_ref if line < half else second_ref
        add_blocks(out, (line % half,), [(mine_ref, (0, line)), (theirs_ref, (0, line))])


def near_kernel(mine_1, mine_2, theirs_1, theirs_2, far_x_ref, far_y_ref, first_ref, second_ref):
    half = far_x_ref.shape[0]
    for line in range(2 * half):
        first = [(mine_1, (0, line)), (theirs_1, (0, line))]
        second = [(mine_2, (0, line)), (theirs_2, (0, line))]
        if line < half:
            second.append((far_x_ref, (line,)))
        else:
            first.append((far_y_ref, (line - half,)))
        add_blocks(first_ref, (line,), first)
        add_blocks(second_ref, (line,), second)


def line_kernel(count, mine_ref, theirs_ref, *refs):
    received, out_refs = refs[:count], refs[count:]
    for line, out in enumerate(out_refs):
        parts = [(mine_ref, (0, line)), (theirs_ref, (0, line))]
        add_blocks(out, (), parts + [(ref, (line,)) for ref in received])


def final_kernel(counts, *refs):
    out_ref = refs[-1]
    at = 0
    for index, count in enumerate(counts):
        add_blocks(out_ref, (index,), [(ref, ()) for ref in refs[at : at + count]])
        at += count


GAIN_ROWS = 16


def gain_terms(gain):
    dims = (GAIN_ROWS, gain.shape[1])
    row = iota(dims, 0)
    rest = jnp.where((row & 1) == 0, gain[0:1, :], gain[1:2, :])
    terms = jnp.zeros(dims, jnp.float32)
    for which in range(3):
        term = wide(to_low(rest))
        terms = jnp.where(lax.shift_right_logical(row, 1) == which, term, terms)
        rest = rest - term
    return to_low(terms)


def last_kernel(gain_ref, *refs):
    out_ref = refs[-1]
    rows = refs[0].shape[0]
    total = refs[0][...]
    for ref in refs[1:-1]:
        total = total + wide(ref[...])
    out_ref[0, :rows] = to_low(total)
    out_ref[0, rows:] = gain_terms(gain_ref[...])


def finish_last(gain, piece, after=()):
    rows, columns = piece[0].shape
    out = shape((1, rows + GAIN_ROWS, columns), jnp.bfloat16)
    args = (gain, *piece)
    return call(
        last_kernel,
        (1,),
        [whole(a) for a in args],
        [whole(out)],
        [out],
        [],
        args,
        out.size,
        after,
        least=0,
    )[0]


def finish(pieces, after=(), least=0):
    out = shape((len(pieces),) + pieces[0][0].shape, jnp.bfloat16)
    args = tuple(a for piece in pieces for a in piece)
    return call(
        functools.partial(final_kernel, tuple(len(piece) for piece in pieces)),
        (1,),
        [whole(a) for a in args],
        [whole(out)],
        [out],
        [],
        args,
        out.size,
        after,
        least=least,
    )[0]


def pair_line_kernel(count, mine_ref, theirs_ref, *refs):
    received, (own_ref, kept_ref, sent_ref) = refs[:count], refs[count:]
    for line in range(4):
        out, at = ((own_ref, ()), (sent_ref, (0,)), (kept_ref, ()), (sent_ref, (1,)))[line]
        parts = [(mine_ref, (0, line)), (theirs_ref, (0, line))]
        add_blocks(out, at, parts + [(ref, (line,)) for ref in received])


def far_line_kernel(own_ref, kept_ref, received_ref, total_ref, sent_ref):
    add_blocks(total_ref, (), [(own_ref, ()), (received_ref, (0,))])
    add_blocks(sent_ref, (), [(kept_ref, ()), (received_ref, (1,))])


class Reduction:
    def __init__(self, place, mine, theirs):
        self.place, self.mine = place, mine
        self.theirs = in_hbm(swap(theirs, "shard", 1))
        self.block = mine.shape[1:]

    def send_plane(self, after=()):
        outs = [shape(self.block, jnp.bfloat16)] * (self.place.groups - 1)
        args = (self.mine,) * len(outs) + (self.theirs,) * len(outs)
        self.sent = call(
            plane_blocks_kernel, (1,),
            [some(self.mine, index % len(outs) + 1, 1) for index in range(len(args))],
            [whole(a) for a in outs], outs, [], args, self.mine.size, after,
        )
        self.plane = [swap(block, "group", mask) for mask, block in enumerate(self.sent, 1)]

    def send(self, kernel, specs, dims, args, after):
        out = shape(dims, jnp.bfloat16)
        return call(
            kernel, (1,), specs, [whole(out)] * 2, [out, out], [], args, self.mine.size, after,

        )

    def send_far(self, after=()):
        args = (self.mine, self.theirs)
        half = (self.block[0] // 2,) + self.block[1:]
        self.sent = self.send(far_kernel, [some(a, 3, 1) for a in args], half, args, after)
        self.far = [swap(self.sent[0], "group", 1), swap(self.sent[1], "group", 2)]

    def send_near(self, after=()):
        args = (self.mine, self.mine, self.theirs, self.theirs, *self.far)
        specs = [some(self.mine, which % 2 + 1, 1) for which in range(4)]
        specs += [whole(a) for a in self.far]
        self.sent = self.send(near_kernel, specs, self.block, args, after)
        self.plane = [swap(self.sent[0], "group", 1), swap(self.sent[1], "group", 2)]

    def send_lines(self, after=()):
        args = (self.mine, self.theirs, *self.plane)
        specs = [some(a, 0, 1) for a in args[:2]] + [whole(a) for a in args[2:]]
        outs = [shape(self.block[1:])]
        outs += [shape(self.block[1:], jnp.bfloat16)] * (self.block[0] - 1)
        self.own, *self.sent_lines = call(
            functools.partial(line_kernel, len(self.plane)), (1,), specs,
            [whole(a) for a in outs], outs, [], args, self.mine.size, after,
        )
        self.lines = swap_blocks(self.sent_lines)

    def send_pair(self, after=()):
        args = (self.mine, self.theirs, *self.plane)
        specs = [some(a, 0, 1) for a in args[:2]] + [whole(a) for a in args[2:]]
        one = self.block[1:]
        outs = [shape(one), shape(one), shape((2,) + one, jnp.bfloat16)]
        self.own, self.kept, self.sent = call(
            functools.partial(pair_line_kernel, len(self.plane)), (1,), specs,
            [whole(a) for a in outs], outs, [], args, self.mine.size, after,
        )
        self.received = swap(self.sent, "shard", 2)

    def send_line(self, after=()):
        args = (self.own, self.kept, self.received)
        outs = [shape(self.own.shape), shape(self.own.shape, jnp.bfloat16)]
        self.own, self.sent = call(
            far_line_kernel, (1,), [whole(a) for a in args], [whole(a) for a in outs], outs, [],
            args, self.own.size, after,
        )
        self.lines = [swap(self.sent, "shard", 4)]


def lines_kernel(*refs):
    count = len(refs) // 3
    for mine_ref, theirs_ref, out in zip(refs[:count], refs[count:], refs[2 * count :]):
        out[0] = to_low(wide(mine_ref[0, 0]) + wide(theirs_ref[0, 0]))


def first_plane_kernel(mine_ref, theirs_ref, *refs):
    received, (own_ref, kept_ref, sent_ref) = refs[:-3], refs[-3:]
    for index in range(4):
        out, at = ((own_ref, ()), (sent_ref, (0,)), (kept_ref, ()), (sent_ref, (1,)))[index]
        parts = [(mine_ref, (0, index)), (theirs_ref, (0, index))]
        add_blocks(out, at, parts + [(ref, (index,)) for ref in received])


class LineReduction:
    def __init__(self, place, mine, theirs):
        self.place, self.mine = place, mine
        self.theirs = in_hbm(swap(theirs, "shard", 1))

    def line_view(self, line):
        block = (1, 1) + self.mine.shape[2:]
        return pl.BlockSpec(block, lambda step: (line, step, 0, 0))

    def send_lines(self, after=()):
        chips, groups, rows, columns = self.mine.shape
        others = range(1, chips)
        out = pl.BlockSpec((1, rows, columns), lambda step: (step, 0, 0))
        self.sent = call(
            lines_kernel, (groups,), [self.line_view(line) for line in others] * 2,
            [out] * len(others), [shape((groups, rows, columns), jnp.bfloat16)] * len(others), [],
            (self.mine,) * len(others) + (self.theirs,) * len(others), self.mine.size, after,
        )
        self.lines = swap_blocks(self.sent)

    def send_first(self, after=()):
        one = self.mine.shape[2:]
        outs = [shape(one), shape(one), shape((2,) + one, jnp.bfloat16)]
        args = (self.mine, self.theirs, *self.lines)
        specs = [some(a, 0, 1) for a in args[:2]] + [whole(a) for a in args[2:]]
        self.own, self.kept, self.sent = call(
            first_plane_kernel, (1,), specs, [whole(a) for a in outs], outs, [],
            args, self.mine.size, after,
        )
        self.received = swap(self.sent, "group", 1)

    def send_second(self, after=()):
        args = (self.own, self.kept, self.received)
        outs = [shape(self.own.shape), shape(self.own.shape, jnp.bfloat16)]
        self.own, self.sent = call(
            far_line_kernel, (1,), [whole(a) for a in args], [whole(a) for a in outs], outs, [],
            args, self.own.size, after,
        )
        self.plane = [swap(self.sent, "group", 2)]


def swap(value, axis, mask):
    size = lax.axis_size(axis)
    return lax.ppermute(value, axis, [(place, place ^ mask) for place in range(size)])


def in_hbm(array):
    return pltpu.with_memory_space_constraint(array, pltpu.MemorySpace.HBM)


def place_at(parts, positions, axis):
    out = jnp.zeros((len(parts),) + parts[0].shape, parts[0].dtype)
    for part, position in zip(parts, positions):
        out = lax.dynamic_update_slice_in_dim(out, part[None], position, 0)
    return out


def gather_piece(piece):
    groups, shards_count = lax.axis_size("group"), lax.axis_size("shard")
    group, shard = lax.axis_index("group"), lax.axis_index("shard")
    far, core = shard // 2, shard % 2
    chips = shards_count // 2
    rows, width = piece.shape
    part_width = width // groups
    own = to_low(lax.dynamic_slice_in_dim(piece, group * part_width, part_width, 1))
    line = [own] + [swap(own, "shard", 2 * mask) for mask in range(1, chips)]
    quarter = place_at(line, [far ^ mask for mask in range(chips)], 0)
    plane = [quarter] + [swap(quarter, "group", mask) for mask in range(1, groups)]
    half = jnp.zeros((chips, rows, width), quarter.dtype)
    for mask in range(groups):
        half = lax.dynamic_update_slice_in_dim(half, plane[mask], (group ^ mask) * part_width, 2)
    other = swap(half, "shard", 1)
    low = jnp.where(core == 0, half, other)
    high = jnp.where(core == 0, other, half)
    return jnp.stack([low, high], axis=1).reshape(shards_count * rows, width)


def reduce_piece(grad):
    groups, shards_count = lax.axis_size("group"), lax.axis_size("shard")
    group, shard = lax.axis_index("group"), lax.axis_index("shard")
    far, core = shard // 2, shard % 2
    chips = shards_count // 2
    width = grad.shape[1]
    rows = grad.shape[0] // shards_count
    part_width = width // groups
    view = grad.reshape(chips, 2, rows, width)
    theirs = to_low(lax.dynamic_index_in_dim(view, 1 - core, 1, keepdims=False))
    mine = lax.dynamic_index_in_dim(view, core, 1, keepdims=False)
    chip_sum = mine.astype(jnp.float32) + swap(theirs, "shard", 1).astype(jnp.float32)

    def columns(which):
        return lax.dynamic_slice_in_dim(chip_sum, which * part_width, part_width, 2)

    plane = [swap(to_low(columns(group ^ mask)), "group", mask) for mask in range(1, groups)]
    plane_sum = columns(group)
    for value in plane:
        plane_sum = plane_sum + value.astype(jnp.float32)

    def line_block(which):
        return lax.dynamic_index_in_dim(plane_sum, which, 0, keepdims=False)

    line = [swap(to_low(line_block(far ^ mask)), "shard", 2 * mask) for mask in range(1, chips)]
    total = line_block(far)
    for value in line:
        total = total + value.astype(jnp.float32)
    total = to_low(total)
    out = jnp.zeros((rows, width), total.dtype)
    for mask in range(groups):
        part = swap(total, "group", mask) if mask else total
        out = lax.dynamic_update_slice_in_dim(out, part, (group ^ mask) * part_width, 1)
    return out


def masks_of(size):
    mask = 1
    while mask < size:
        yield mask
        mask *= 2


def sum_over(value, axis):
    for mask in masks_of(lax.axis_size(axis)):
        value = value + swap(value, axis, mask)
    return value


def spread_columns(array):
    count = lax.axis_size("shard")
    columns = array.shape[1]
    out = jnp.zeros((array.shape[0], columns * count), array.dtype)
    return lax.dynamic_update_slice_in_dim(out, array, lax.axis_index("shard") * columns, 1)


def own_columns(array):
    columns = array.shape[1] // lax.axis_size("shard")
    return lax.dynamic_slice_in_dim(array, lax.axis_index("shard") * columns, columns, 1)


def gather_embeds(low):
    value = low
    shard, group = lax.axis_index("shard"), lax.axis_index("group")
    steps = [("shard", mask, shard) for mask in masks_of(lax.axis_size("shard")) if mask > 1]
    steps += [("group", mask, group) for mask in masks_of(lax.axis_size("group"))]
    steps += [("shard", 1, shard)]
    for axis, mask, index in steps:
        other = swap(value, axis, mask)
        upper = (index & mask) != 0
        value = jnp.concatenate(
            [jnp.where(upper, other, value), jnp.where(upper, value, other)], axis=0
        )
    return value


def shards(
    image_states,
    text_states,
    image_weights,
    image_gains,
    text_weights,
    text_gains,
    logit_scale,
    pair_ids,
    row_stats,
    col_stats,
    gain_stats,
):
    rows, model_width = text_weights.shape[0], text_states.shape[1]
    hidden = (text_weights.shape[1] - 4 * model_width) // 2
    bounds = (
        0,
        3 * model_width,
        4 * model_width,
        4 * model_width + hidden,
        4 * model_width + 2 * hidden,
    )
    groups, chips = lax.axis_size("group"), lax.axis_size("shard") // 2
    group, shard = lax.axis_index("group"), lax.axis_index("shard")
    pos = jnp.stack([shard // 2, shard % 2, group]).astype(jnp.int32)
    own_pairs = pair_ids.shape[0]
    scale = logit_scale.reshape(1, 1)
    place = None
    if rows % 16 == 0 and groups == 4 and chips == 4 and hidden == 4 * model_width:
        place = Place(chips, rows, groups)

    rounded_gains = lax.reduce_precision(text_gains, exponent_bits=8, mantissa_bits=7)
    gain_rows = jnp.concatenate([rounded_gains, gain_stats])
    gain_rows = spread_columns(gain_rows)
    lead = ()
    if place is not None:
        width = hidden // groups
        own_first, own_up, own_down = cut(text_weights, groups, width, pos)
        line = line_gather(own_first, chips)
        high_up = swap(own_up, "shard", 4)
    class_rows = image_attention(image_states, image_weights, image_gains)
    if place is not None:
        quarter, own_down, gain_rows = arrange(
            [[(k, 0, 1) for k in range(4)], [(4, 0, 2)], [(5, 0, 1)]],
            (*line, own_down, gain_rows[None]),
            after=(class_rows,),
        )
        first_piece = RelayGather(place, (0, 1, 2, 3), quarter, hidden)
        gain_rows = gain_rows + swap(gain_rows, "shard", 1)
        pair, gain_rows = arrange(
            [[(0, 0, 2), (1, 0, 2)], [(2, 0, 1)]], (own_up, high_up, gain_rows), (quarter,)
        )
        gain_rows = gain_rows + swap(gain_rows, "shard", 2)
        low_up = swap(pair, "shard", 2)
        high_down = swap(own_down, "shard", 4)
        lead = (quarter, pair)
    image_embed, image_low = image_mlp(
        class_rows, image_weights, image_gains, own_pairs, after=lead
    )
    padded = image_low.shape[0]
    total_pairs = padded * groups * chips * 2
    image_bias = np.where(np.arange(total_pairs) % padded < own_pairs, 0.0, MASKED)
    image_bias = jnp.asarray(image_bias[None], jnp.float32)

    if place is None:
        for mask in masks_of(2 * chips):
            gain_rows = gain_rows + swap(gain_rows, "shard", mask)
        gains, all_gain_stats = gain_rows[:2], gain_rows[2:]
        w_first, w_up, w_down = (
            Weights(None, [gather_piece(text_weights[:, lower:upper])[None]], None, upper - lower)
            for lower, upper in ((0, bounds[2]), bounds[2:4], bounds[3:5])
        )
        images = Weights(None, [gather_embeds(image_low)[None]], None, model_width)
        own_block = (shard % 2) * (groups * chips) + group * chips + shard // 2
        qkv, full_first = project(text_states, w_first, gains, pos)
        mixed, first = attention_forward(text_states, qkv, full_first)
        hidden_sum, slope, pooled, full_up = up_forward(first, w_up, gains, pos)
    else:
        own_block = shard * groups + group
        order = (0, 2, 1, 3)
        masks = tuple(range(groups))

        def quarter_plan(which, at):
            plan = [(at, which, which + 1), (at + 1, which, which + 1)]
            return plan + [(at + 2, which, which + 1), (at + 2, which + 2, which + 3)]

        join_plan = [(k, 0, chips) for k in masks]
        half = chips // 2
        far_x, far_y, joined, *quarters, image_own, gain_rows = arrange(
            first_piece.plan() + [quarter_plan(0, 3), quarter_plan(1, 3), [(6, 0, 1)], [(7, 0, 1)]],
            (*first_piece.blocks, own_up, high_up, low_up, image_low[None], gain_rows),
        )
        first_piece.send_far(far_x, far_y, joined)
        image_high = swap(image_own, "shard", 4)
        corner, *quarters, gain_rows, image_pair, pair = arrange(
            [[(0, 0, half), (1, 0, half)], [(2, 0, chips)], [(3, 0, chips)]]
            + [[(4, 0, 1)], [(5, 0, 1), (6, 0, 1)], [(7, 0, 2), (8, 0, 2)]],
            (
                *first_piece.far, *quarters, gain_rows, image_own, image_high,
                own_down, high_down,
            ),
        )
        low_down = swap(pair, "shard", 2)
        w_first = first_piece.weights(corner)
        up_piece = Gather(place, order, quarters, hidden)
        image_lower = swap(image_pair, "shard", 2)
        gain_rows = (gain_rows + swap(gain_rows, "shard", 4))[0]
        gains, all_gain_stats = gain_rows[:2], gain_rows[2:]
        qkv, full_first = project(text_states, w_first, gains, pos)
        (image_quarter,) = arrange(
            [[(0, 0, 2), (1, 0, 2)]], (image_pair, image_lower), after=(qkv,)
        )
        image_blocks = [image_quarter] + [swap(image_quarter, "group", mask) for mask in (1, 2)]
        mixed, first = attention_forward(text_states, qkv, full_first, after=(image_quarter,))
        joined, far_x, far_y, *quarters = arrange(
            [join_plan, [(groups, 0, half)], [(groups + 1, half, chips)]]
            + [quarter_plan(0, groups + 2), quarter_plan(1, groups + 2)],
            (*up_piece.blocks, *image_blocks[1:], own_down, high_down, low_down),
            after=(first,),
        )
        image_blocks += [swap(far_x, "group", 2), swap(far_y, "group", 1)]
        w_up = up_piece.weights(joined)
        down_piece = Gather(place, order, quarters, hidden)
        hidden_sum, slope, pooled, full_up = up_forward(
            first, w_up, gains, pos, after=tuple(quarters)
        )
        joined, image_joined = arrange(
            [join_plan]
            + [[(groups + k, 0, chips) for k in (0, 1, 2)] + [(7, 0, half), (8, 0, half)]],
            (*down_piece.blocks, *image_blocks),
            after=(hidden_sum,),
        )
        w_down = down_piece.weights(joined)
        images = Weights(
            Place(chips, padded, groups, stacked=True),
            image_blocks + [in_hbm(swap(image_joined, "shard", 1))],
            [(order, (mask,), True) for mask in (0, 1, 2)]
            + [(order[:half], (3,), True), (order[half:], (3,), True), (order, masks, False)],
            model_width,
        )
    text_embed, pooled_inv, scores, row_total, col_total, full_down, all_image = scores_forward(
        hidden_sum, pooled, w_down, images, image_bias, scale, pos
    )
    norm_up = turned_norm(first, gains, 1, after=(col_total,))
    if place is None:
        rounds = [(axis, (mask,)) for axis in ("shard", "group") for mask in masks_of(lax.axis_size(axis))]
    else:
        rounds = [("shard", (1,)), ("shard", (2, 4, 6)), ("group", (1, 2, 3))]
    for axis, near in rounds:
        received = [swap(col_total, axis, mask) for mask in near]
        for value in received:
            col_total = jnp.logaddexp(col_total, value)
    target = (own_block * padded + pair_ids)[:, None]
    grad_hidden, grad_out, grads_down = scores_backward(
        scores, row_total, col_total, target, scale, all_image, text_embed, pooled_inv,
        hidden_sum, full_down, place, pos, after=(norm_up,),
    )
    norm_first = turned_norm(text_states, gains, 0, after=(grad_out,))
    after = [()] * 4
    if place is not None:
        down = Reduction(place, *grads_down)
        down.send_plane(after=(norm_first,))
        after[0] = tuple(down.sent)
    grad_b, grads_up = up_backward(
        grad_hidden, slope, norm_up, full_up, place, pos, after=after[0]
    )
    grad_first, grad_low, grad_mixed, grad_gain_up = first_backward(
        grad_b, grad_out, first, gains, full_first
    )
    if place is not None:
        up = Reduction(place, *grads_up)
        up.send_far(after=(grad_low,))
        after[1] = tuple(up.sent)
    grad_qkv = attention_backward(qkv, grad_mixed, after=after[1])
    if place is not None:
        down.send_pair(after=(grad_qkv,))
        up.send_near(after=(down.sent,))
        after[2] = tuple(up.sent)
    grads_first = first_weight(norm_first, mixed, grad_low, grad_qkv, place, pos, after=after[2])
    if place is not None:
        last = Reduction(place, *grads_first)
        after[3] = (grads_first[0],)
    grad_states, grad_gain_first = states_backward(
        grad_qkv, grad_first, text_states, gains, full_first, after=after[3]
    )
    gain_total = jnp.concatenate([grad_gain_first, grad_gain_up], axis=0)
    if place is not None:
        last.send_plane(after=(grad_states,))
        up.send_pair(after=tuple(last.sent))
        down.send_line(after=(up.sent,))
        up.send_line(after=(down.sent,))
        others = finish([[up.own] + up.lines, [down.own] + down.lines])
        near = [swap(others, "group", mask) for mask in (1, 2)]
        last.send_lines(after=(others,))
        result = finish_last(gain_total, [last.own] + last.lines)
        pieces = [(result, 0)] + [
            (swap(result, "group", mask), 0) for mask in range(1, groups)
        ]
        blocks = [others, *near, swap(near[0], "group", 2)]
        pieces += [(block, which) for which in (0, 1) for block in blocks]
    else:
        gain_total = sum_over(gain_total, "group")
        pieces = [
            (reduce_piece(grads[0])[None], 0) for grads in (grads_first, grads_up, grads_down)
        ]
    weight_grad, new_rows, sums = gradient_stats(
        pieces, row_stats, gain_total, bounds, place, pos
    )
    sums = sum_over(sums, "shard")
    new_weights, new_low, new_cols, ratios, gain_grad, new_gain_stats, gain_update = (
        update_weights(
            in_hbm(weight_grad), in_hbm(text_weights), sums, col_stats, new_rows, all_gain_stats,
            bounds,
        )
    )
    new_gains = text_gains - own_columns(gain_update)
    return (
        text_embed,
        image_embed,
        grad_states,
        weight_grad,
        new_rows.T,
        new_cols.reshape(-1),
        new_weights,
        new_low,
        own_columns(gain_grad),
        own_columns(new_gain_stats),
        new_gains,
        to_low(new_gains),
        ratios[0],
    )


def solution(mesh):
    in_specs = (
        P(("group", "shard"), None),
        P(("group", "shard"), None),
        P(),
        P(),
        P("shard", None),
        P(None, "shard"),
        P(),
        P(("group", "shard")),
        P(None, "shard"),
        P(),
        P(None, "shard"),
    )
    out_specs = (
        P(("group", "shard"), None),
        P(("group", "shard"), None),
        P(("group", "shard"), None),
        P("shard", None),
        P(None, "shard"),
        P(),
        P("shard", None),
        P("shard", None),
        P(None, "shard"),
        P(None, "shard"),
        P(None, "shard"),
        P(None, "shard"),
        P(),
    )
    return jax.shard_map(shards, mesh=mesh, in_specs=in_specs, out_specs=out_specs, check_vma=False)
```
